512 devices in a mesh: chan: 64 (over y, x, core), rad: 8 (over z).
Axes of the slice: x: 4, y: 8, z: 8, core: 2. Of those that a mesh axis runs over, the one named last changes fastest.
Arguments:
- trial: bfloat16 [64, 256, 2048], P(None, 'chan', 'rad')
- band: bfloat16 [256, 17, 2048], P('chan', None, 'rad'), may hold values from -1.5 to 1.5
- band_width: int32 [256], P('chan'), may hold values from 1 to 8
- energies: float32 [256], P('chan'), may hold values from 0.5 to 8
- coupling: bfloat16 [2048, 2048, 256], P('chan', 'rad')
- reach: int32 [2048], P('chan'), may hold values from 1 to 8
- pair_target: int32 [2048], P('chan'), may hold values from 0 to 255, as said below
- pair_source: int32 [2048], P('chan'), may hold values from 0 to 255, as said below
- chan_slot: int32 [256], replicated, may hold values from 0 to 255, as said below
Outputs:
- residual: bfloat16 [64, 256, 2048], P(None, 'chan', 'rad')
- rayleigh: float32 [64, 64], replicated
The draws below stay inside these ranges and needn't reach their ends.
Inputs may be any that keep to these rules, and one draw needn't show every extreme that they name: A permutation: channel c's rows stand at slot chan_slot[c]. `pair_target`: the pairs of block t of 32 pairs target channels whose slots lie in t * 4 to t * 4 + 3. `pair_source`: in each block of 32 pairs, at most 1 pair has its source slot in any one aligned group of 4 slots (so the 32 sources lie in 32 different groups).
All inputs are finite; a program needn't handle non-finite values.
Results may differ from the reference program's by a relative error of at most 0.0061.
Values may be sent and summed in bfloat16 or wider, within the bound.
No kernel may reach another device: no remote copies, remote signals or barrier semaphores. Data moves between devices by JAX's collectives and lax.ppermute only.
A program may use at most 64 MiB of HBM per device.

```python
import math
import jax
import jax.numpy as jnp
from jax import lax

K = 64
NB = 2048
CH_DEV = 4
BW = 8
BLK = 256
PAIRS_DEV = 32
CAP = 1
CHANNELS = 256
PAIRS = 2048


def layout(key):
    device_count = CHANNELS // CH_DEV
    slot_of = jax.random.permutation(jax.random.fold_in(key, 11), CHANNELS).astype(jnp.int32)
    channel_at = jnp.argsort(slot_of, stable=True).astype(jnp.int32)
    key_list = jax.random.split(jax.random.fold_in(key, 13), device_count)

    def per_device(dev_key):
        owners = jax.random.permutation(jax.random.fold_in(dev_key, 1), device_count).astype(jnp.int32)
        positions = jax.random.permutation(jax.random.fold_in(dev_key, 2), CAP * device_count)[:PAIRS_DEV].astype(jnp.int32)
        source_dev = owners[positions % device_count]
        source_local = jax.random.randint(jax.random.fold_in(dev_key, 4), (PAIRS_DEV,), 0, CH_DEV).astype(jnp.int32)
        target_local = jax.random.randint(jax.random.fold_in(dev_key, 5), (PAIRS_DEV,), 0, CH_DEV).astype(jnp.int32)
        return (source_dev * CH_DEV + source_local, target_local)
    source_slots, target_locals = jax.vmap(per_device)(key_list)
    target_slots = jnp.arange(device_count, dtype=jnp.int32)[:, None] * CH_DEV + target_locals
    return (slot_of, channel_at[target_slots.reshape(-1)], channel_at[source_slots.reshape(-1)])


def draw_chan_slot(key, part):
    return layout(key)[0]


def draw_pair_target(key, part):
    return layout(key)[1]


def draw_pair_source(key, part):
    return layout(key)[2]


def draw_trial(key, part):
    shape = (K, CHANNELS, NB)
    noise = jax.random.normal(jax.random.fold_in(key, 1), shape, jnp.float32)
    shared_weight = 0.5
    common = jax.random.normal(jax.random.fold_in(key, 5), (K, 1, NB), jnp.float32)
    shared = jax.random.normal(jax.random.fold_in(key, 6), (1, CHANNELS, NB), jnp.float32)
    mixed = noise + 0.5 * common + shared_weight * shared
    chan_pos = jnp.arange(CHANNELS, dtype=jnp.float32) / CHANNELS
    rad_pos = jnp.arange(NB, dtype=jnp.float32) / NB
    jitter = jax.random.uniform(jax.random.fold_in(key, 3), (CHANNELS, NB), jnp.float32)
    row_scale = 0.06 * jnp.power(10.0, 1.2 * (1.0 - chan_pos[:, None]) + 0.25 * rad_pos[None, :] + 0.3 * jitter)
    col_scale = jnp.power(10.0, jax.random.uniform(jax.random.fold_in(key, 4), (K,), jnp.float32, -0.3, 0.3))
    return (mixed * row_scale[None] * col_scale[:, None, None]).astype(jnp.bfloat16)


def draw_coupling(key, part):
    key = jax.random.fold_in(key, 29)
    noise = jax.random.normal(jax.random.fold_in(key, 1), (PAIRS, NB, BLK), jnp.float32) * (1.0 / math.sqrt(BLK))
    strength = jax.random.uniform(jax.random.fold_in(key, 2), (PAIRS, 1, 1), jnp.float32, 0.3, 0.7)
    row_pos = jnp.arange(NB, dtype=jnp.int32) % BLK
    diagonal = (row_pos[:, None] == jnp.arange(BLK, dtype=jnp.int32)[None, :]).astype(jnp.float32)
    return (noise + strength * diagonal[None]).astype(jnp.bfloat16)


def set_ends(drawn, rng, smallest, largest):
    dims = drawn.shape
    spot = [jax.random.randint(jax.random.fold_in(rng, axis), (), 0, dims[axis]) for axis in range(len(dims))]
    drawn = drawn.at[tuple(spot)].set(smallest)
    longest = dims.index(max(dims))
    spot[longest] = (spot[longest] + 1) % dims[longest]
    return drawn.at[tuple(spot)].set(largest)


def shard_levels(stream_key, shape, pieces, least, largest):
    gain = 1.0
    for position, blocks in pieces:
        draws = jax.random.uniform(jax.random.fold_in(jax.random.fold_in(stream_key, 6), position), (blocks,), jnp.float32, least / len(pieces), largest / len(pieces))
        gain = gain * jnp.repeat(jnp.exp(draws), shape[position] // blocks).reshape((-1,) + (1,) * (len(shape) - 1 - position))
    return gain


def scatter_about(rng, shape, deviation, bound, pieces=(), kind=jnp.bfloat16):
    drawn = deviation * jax.random.normal(rng, shape, jnp.float32)
    if pieces:
        drawn = drawn * shard_levels(rng, shape, pieces, -0.22, 0.18)
    return jnp.clip(drawn, -bound, bound).astype(kind)


def setup_inputs(seed: int = 0) -> dict:
    seeds = jax.random.split(jax.random.key(seed), 10)
    return {
        "trial": draw_trial(jax.random.fold_in(seeds[9], 71), 0),
        "band": scatter_about(seeds[1], (CHANNELS, 2 * BW + 1, NB), 0.3, 1.5, ((0, 64), (2, 8))),
        "band_width": set_ends(jax.random.randint(seeds[2], (CHANNELS,), 1, BW + 1), jax.random.fold_in(seeds[2], 1), 1, BW).astype(jnp.int32),
        "energies": jnp.clip(jnp.exp(math.log(8.0) - 2.7725887 * jax.random.uniform(seeds[3], (CHANNELS,), jnp.float32) ** shard_levels(seeds[3], (CHANNELS,), ((0, 64),), -0.2, 0.2)), 0.5, 8.0),
        "coupling": draw_coupling(jax.random.fold_in(seeds[9], 71), 0),
        "reach": set_ends(jax.random.randint(seeds[5], (PAIRS,), 1, NB // BLK + 1), jax.random.fold_in(seeds[5], 1), 1, (NB // BLK + 1) - 1).astype(jnp.int32),
        "pair_target": draw_pair_target(jax.random.fold_in(seeds[9], 71), 0),
        "pair_source": draw_pair_source(jax.random.fold_in(seeds[9], 71), 0),
        "chan_slot": draw_chan_slot(jax.random.fold_in(seeds[9], 71), 0),
    }


def reference(trial, band, band_width, energies, coupling, reach, pair_target, pair_source, chan_slot):
    padded = jnp.pad(trial, ((0, 0), (0, 0), (BW, BW)))
    running = energies[None, :, None] * trial.astype(jnp.float32)
    for offset in range(2 * BW + 1):
        live_mask = (abs(offset - BW) <= band_width).astype(jnp.float32)
        running = running + (live_mask[:, None] * band[:, offset, :].astype(jnp.float32))[None] * padded[:, :, offset:offset + NB].astype(jnp.float32)
    source_slot = chan_slot[pair_source].astype(jnp.int32)
    target_slot = chan_slot[pair_target].astype(jnp.int32)
    intervals = NB // BLK

    def one_pair(total, inputs):
        matrix, source, target, extent = inputs
        vector = lax.dynamic_index_in_dim(trial, source, 1, keepdims=False).astype(jnp.float32).reshape(K, intervals, BLK)
        blocks = matrix.astype(jnp.float32).reshape(intervals, BLK, BLK)
        coupled = jnp.einsum('bij,kbj->kbi', blocks, vector, precision=lax.Precision.HIGHEST)
        reach_mask = (jnp.arange(intervals, dtype=jnp.int32) < extent).astype(jnp.float32)
        coupled = (coupled * reach_mask[None, :, None]).reshape(K, NB)
        current = lax.dynamic_index_in_dim(total, target, 1, keepdims=False)
        total = lax.dynamic_update_index_in_dim(total, current + coupled, target, 1)
        return (total, None)
    running, _ = lax.scan(one_pair, running, (coupling, source_slot, target_slot, reach))
    image = running.astype(jnp.bfloat16)
    trial_wide = trial.astype(jnp.float32)
    gram = jnp.einsum('kcr,lcr->kl', trial_wide, trial_wide, precision=lax.Precision.HIGHEST)
    projected = jnp.einsum('kcr,lcr->kl', trial_wide, image.astype(jnp.float32), precision=lax.Precision.HIGHEST)
    factor = jnp.linalg.cholesky(gram)
    halfway = lax.linalg.triangular_solve(factor, projected, left_side=True, lower=True)
    rayleigh = lax.linalg.triangular_solve(factor, halfway, left_side=True, lower=True, transpose_a=True)
    rounded = rayleigh.astype(jnp.bfloat16)
    residual = image.astype(jnp.float32) - jnp.einsum('kcr,kl->lcr', trial_wide, rounded.astype(jnp.float32), precision=lax.Precision.HIGHEST)
    return (residual.astype(jnp.bfloat16), rayleigh)
```

```python
import functools

import jax
import jax.numpy as jnp
from jax import lax
from jax.experimental import pallas as pl
from jax.experimental.pallas import tpu as pltpu
from jax.sharding import Mesh, PartitionSpec as P

BW = 8
BLK = 256
CORES = 2
X_CHIPS = 4
VMEM = pl.BlockSpec(memory_space=pltpu.VMEM)
SMEM = pl.BlockSpec(memory_space=pltpu.SMEM)
NT = (((1,), (1,)), ((), ()))
HIGH = lax.Precision.HIGHEST
PARAMS = pltpu.CompilerParams(vmem_limit_bytes=40 * 1024 * 1024)


def pick_kernel(per_group, want, rows, out):
    @pl.loop(0, out.shape[0])
    def _(i):
        group = lax.rem(i, rows.shape[0] // per_group)
        out[i] = rows[group * per_group + want[i]]


def image_kernel(slot, target, live, rows, coupling, banded, trial, image, proj, total):
    total[...] = banded[...]

    @pl.loop(0, coupling.shape[0])
    def _(p):
        part = lax.dot_general(
            rows[slot[p]], coupling[p], NT, preferred_element_type=jnp.float32
        )
        total[target[p]] += part * live[p]

    acc = jnp.zeros(proj.shape, jnp.float32)
    for c in range(total.shape[0]):
        rounded = total[c].astype(jnp.bfloat16)
        image[c] = rounded
        acc += lax.dot_general(trial[c], rounded, NT, preferred_element_type=jnp.float32)
    proj[...] = acc


def residual_kernel(inverse, projected, trial, image, residual, rayleigh):
    inv = inverse[...]
    half = jnp.dot(inv, projected[...], precision=HIGH, preferred_element_type=jnp.float32)
    full = lax.dot_general(
        inv, half, (((0,), (0,)), ((), ())), precision=HIGH, preferred_element_type=jnp.float32
    )
    rayleigh[...] = full
    flipped = full.T.astype(jnp.bfloat16)
    for c in range(trial.shape[0]):
        fit = jnp.dot(flipped, trial[c], preferred_element_type=jnp.float32)
        residual[c] = (image[c].astype(jnp.float32) - fit).astype(jnp.bfloat16)


def total_of(part):
    size = part.shape[0]
    inner = lax.axis_size("x") * lax.axis_size("core")
    outer = lax.axis_size("y") * lax.axis_size("rad")
    pieces = part.reshape(inner, size // inner, size)
    mine = jnp.sum(lax.all_to_all(pieces, ("x", "core"), 0, 0, tiled=True), axis=0)
    spread = jnp.broadcast_to(mine[None], (outer,) + mine.shape)
    mine = jnp.sum(lax.all_to_all(spread, ("y", "rad"), 0, 0, tiled=True), axis=0)
    spread = jnp.broadcast_to(mine[None], (inner,) + mine.shape)
    return lax.all_to_all(spread, ("x", "core"), 0, 0, tiled=True).reshape(size, size)


def lookup(table, wanted_ids):
    match = wanted_ids[:, None] == jnp.arange(table.shape[0], dtype=jnp.int32)[None, :]
    return jnp.sum(jnp.where(match, table[None, :], 0), axis=1)


def body(trial, band, band_width, energies, coupling, reach, pair_target, pair_source, chan_slot):
    vecs, slots, slab = trial.shape
    ys, xs, cores, slabs = (lax.axis_size(a) for a in ("y", "x", "core", "rad"))
    me = (lax.axis_index("y") * xs + lax.axis_index("x")) * cores + lax.axis_index("core")
    columns = xs * cores

    source_slot = lookup(chan_slot, pair_source)
    target_local = lookup(chan_slot, pair_target) - me * slots
    group = source_slot // slots
    member = source_slot - group * slots
    hit = group[:, None] == jnp.arange(ys * columns, dtype=jnp.int32)[None, :]
    need = jnp.sum(jnp.where(hit, member[:, None], 0), axis=0).reshape(ys, columns)
    want = lax.all_to_all(need.T, ("x", "core"), 0, 0, tiled=True).reshape(-1)
    where_held = lax.rem(group, columns) * ys + group // columns
    live = (lax.axis_index("rad") < reach).astype(jnp.float32)

    by_slot = jnp.transpose(trial, (1, 0, 2))
    column = lax.all_gather(by_slot, "y", axis=0, tiled=True)
    picked = pl.pallas_call(
        functools.partial(pick_kernel, slots),
        out_shape=jax.ShapeDtypeStruct((columns * ys, vecs, slab), jnp.bfloat16),
        in_specs=[SMEM, VMEM],
        out_specs=VMEM,
        compiler_params=PARAMS,
        name="pick",
    )(want, column)
    rows = lax.all_to_all(picked, ("x", "core"), 0, 0, tiled=True)

    gram = total_of(
        lax.dot_general(
            trial, trial, (((1, 2), (1, 2)), ((), ())), preferred_element_type=jnp.float32
        )
    )
    factor = jnp.linalg.cholesky(gram)
    inverse = lax.linalg.triangular_solve(
        factor, jnp.eye(vecs, dtype=jnp.float32), left_side=True, lower=True
    )

    up = [(i, i + 1) for i in range(slabs - 1)]
    before = lax.ppermute(by_slot[:, :, slab - BW :], "rad", up)
    after = lax.ppermute(by_slot[:, :, :BW], "rad", [(j, i) for i, j in up])
    padded = jnp.concatenate([before, by_slot, after], axis=2)
    banded = energies[:, None, None] * by_slot.astype(jnp.float32)
    for offset in range(2 * BW + 1):
        inside = (abs(offset - BW) <= band_width).astype(jnp.float32)
        weight = inside[:, None] * band[:, offset, :].astype(jnp.float32)
        banded += weight[:, None] * padded[:, :, offset : offset + slab].astype(jnp.float32)

    image, part = pl.pallas_call(
        image_kernel,
        out_shape=(
            jax.ShapeDtypeStruct(by_slot.shape, jnp.bfloat16),
            jax.ShapeDtypeStruct((vecs, vecs), jnp.float32),
        ),
        in_specs=[SMEM, SMEM, SMEM, VMEM, VMEM, VMEM, VMEM],
        out_specs=(VMEM, VMEM),
        scratch_shapes=[pltpu.VMEM(by_slot.shape, jnp.float32)],
        compiler_params=PARAMS,
        name="image",
    )(where_held, target_local, live, rows, coupling, banded, by_slot)
    projected = total_of(part)
    residual, rayleigh = pl.pallas_call(
        residual_kernel,
        out_shape=(
            jax.ShapeDtypeStruct(by_slot.shape, jnp.bfloat16),
            jax.ShapeDtypeStruct((vecs, vecs), jnp.float32),
        ),
        in_specs=[VMEM] * 4,
        out_specs=(VMEM, VMEM),
        compiler_params=PARAMS,
        name="residual",
    )(inverse, projected, by_slot, image)
    return jnp.transpose(residual, (1, 0, 2)), rayleigh


def solution(mesh):
    chan, rad = mesh.shape["chan"], mesh.shape["rad"]
    fine = Mesh(
        mesh.devices.reshape(chan // (X_CHIPS * CORES), X_CHIPS, CORES, rad),
        ("y", "x", "core", "rad"),
    )
    over = ("y", "x", "core")
    placed = (
        P(None, over, "rad"),
        P(over, None, "rad"),
        P(over),
        P(over),
        P(over, "rad", None),
        P(over),
        P(over),
        P(over),
        P(),
    )
    return jax.shard_map(
        body, mesh=fine, in_specs=placed, out_specs=(P(None, over, "rad"), P()), check_vma=False
    )
```

```python
import functools

import jax
import jax.numpy as jnp
from jax import lax
from jax.experimental import pallas as pl
from jax.experimental.pallas import tpu as pltpu
from jax.sharding import Mesh, PartitionSpec as P

BW = 8
BLK = 256
CORES = 2
X_CHIPS = 4
UNROLL = 8
DIRECT = 16
CHAN = ("y", "x", "core")
VMEM = pl.BlockSpec(memory_space=pltpu.VMEM)
SMEM = pl.BlockSpec(memory_space=pltpu.SMEM)
NT = (((1,), (1,)), ((), ()))
HIGH = lax.Precision.HIGHEST
PARAMS = pltpu.CompilerParams(vmem_limit_bytes=40 * 1024 * 1024)


def pick_kernel(per_group, want, rows, out):
    @pl.loop(0, out.shape[0])
    def _(i):
        group = lax.rem(i, rows.shape[0] // per_group)
        out[i] = rows[group * per_group + want[i]]


def pack(square):
    half = square.shape[0] // 2
    return jnp.concatenate([square[:half], square[half:]], axis=1)


def unpack(packed):
    half = packed.shape[1] // 2
    return jnp.concatenate([packed[:, :half], packed[:, half:]], axis=0)


def gram_kernel(trial, gram):
    acc = jnp.zeros((trial.shape[1], trial.shape[1]), jnp.float32)
    for c in range(trial.shape[0]):
        acc += lax.dot_general(trial[c], trial[c], NT, preferred_element_type=jnp.float32)
    gram[...] = pack(acc)


def image_kernel(
    slot, group, target, live, relayed, direct, coupling, banded, trial, image, proj, total
):
    total[...] = banded[...]

    @pl.loop(0, coupling.shape[0], step=UNROLL)
    def _(first):
        for i in range(UNROLL):
            p = first + i
            rows = jnp.concatenate([relayed[slot[p]], direct[group[p]]], axis=0)
            part = lax.dot_general(rows, coupling[p], NT, preferred_element_type=jnp.float32)
            total[target[p]] += part * live[p]

    acc = jnp.zeros((trial.shape[1], trial.shape[1]), jnp.float32)
    for c in range(total.shape[0]):
        rounded = total[c].astype(jnp.bfloat16)
        image[c] = rounded
        acc += lax.dot_general(trial[c], rounded, NT, preferred_element_type=jnp.float32)
    proj[...] = pack(acc)


def residual_kernel(inverse, projected, trial, image, residual, rayleigh):
    inv = inverse[...]
    half = jnp.dot(inv, unpack(projected[...]), precision=HIGH, preferred_element_type=jnp.float32)
    full = lax.dot_general(
        inv, half, (((0,), (0,)), ((), ())), precision=HIGH, preferred_element_type=jnp.float32
    )
    rayleigh[...] = full
    flipped = full.T.astype(jnp.bfloat16)
    for c in range(trial.shape[0]):
        fit = jnp.dot(flipped, trial[c], preferred_element_type=jnp.float32)
        residual[c] = (image[c].astype(jnp.float32) - fit).astype(jnp.bfloat16)


def scatter(packed, axes):
    count = lax.axis_size(axes)
    pieces = packed.reshape(count, packed.shape[0] // count, packed.shape[1])
    return jnp.sum(lax.all_to_all(pieces, axes, 0, 0, tiled=True), axis=0)


def exchange(piece, axes):
    spread = jnp.broadcast_to(piece[None], (lax.axis_size(axes),) + piece.shape)
    return lax.all_to_all(spread, axes, 0, 0, tiled=True)


def gather(piece, axes):
    return exchange(piece, axes).reshape(-1, piece.shape[1])


def pick(want, rows, per_group):
    return pl.pallas_call(
        functools.partial(pick_kernel, per_group),
        out_shape=jax.ShapeDtypeStruct(want.shape + rows.shape[1:], rows.dtype),
        in_specs=[SMEM, VMEM],
        out_specs=VMEM,
        compiler_params=PARAMS,
        name="pick",
    )(want, rows)


def lookup(table, wanted_ids):
    match = wanted_ids[:, None] == jnp.arange(table.shape[0], dtype=jnp.int32)[None, :]
    return jnp.sum(jnp.where(match, table[None, :], 0), axis=1)


def body(trial, band, band_width, energies, coupling, reach, pair_target, pair_source, chan_slot):
    vecs, slots, slab = trial.shape
    ys, xs, cores, slabs = (lax.axis_size(a) for a in ("y", "x", "core", "rad"))
    me = (lax.axis_index("y") * xs + lax.axis_index("x")) * cores + lax.axis_index("core")
    columns = xs * cores
    relays = vecs - DIRECT

    source_slot = lookup(chan_slot, pair_source)
    target_local = lookup(chan_slot, pair_target) - me * slots
    group = source_slot // slots
    member = source_slot - group * slots
    hit = group[:, None] == jnp.arange(ys * columns, dtype=jnp.int32)[None, :]
    need = jnp.sum(jnp.where(hit, member[:, None], 0), axis=0)
    want = lax.all_to_all(need.reshape(ys, columns).T, ("x", "core"), 0, 0, tiled=True)
    want_direct = lax.all_to_all(need[:, None], CHAN, 0, 0, tiled=True)
    slot = lax.rem(group, columns) * ys + group // columns
    live = (lax.axis_index("rad") < reach).astype(jnp.float32)

    by_slot = jnp.transpose(trial, (1, 0, 2))
    column = lax.all_gather(by_slot[:, :relays], "y", axis=0, tiled=True)
    straight = lax.all_to_all(
        pick(want_direct.reshape(-1), by_slot[:, relays:], slots), CHAN, 0, 0, tiled=True
    )
    gram = pl.pallas_call(
        gram_kernel,
        out_shape=jax.ShapeDtypeStruct((vecs // 2, 2 * vecs), jnp.float32),
        in_specs=[VMEM],
        out_specs=VMEM,
        compiler_params=PARAMS,
        name="gram",
    )(by_slot)
    piece = scatter(gram, "rad")
    piece = jnp.sum(exchange(piece, ("x", "core")), axis=0)
    picked = pick(want.reshape(-1), column, slots)
    piece, picked = lax.optimization_barrier((piece, picked))
    relayed = lax.all_to_all(picked, ("x", "core"), 0, 0, tiled=True)
    piece = jnp.sum(exchange(piece, "y"), axis=0)
    factor = jnp.linalg.cholesky(unpack(gather(piece, "rad")))
    inverse = lax.linalg.triangular_solve(
        factor, jnp.eye(vecs, dtype=jnp.float32), left_side=True, lower=True
    )

    up = [(i, i + 1) for i in range(slabs - 1)]
    before = lax.ppermute(by_slot[:, :, slab - BW :], "rad", up)
    after = lax.ppermute(by_slot[:, :, :BW], "rad", [(j, i) for i, j in up])
    padded = jnp.concatenate([before, by_slot, after], axis=2)
    banded = energies[:, None, None] * by_slot.astype(jnp.float32)
    for offset in range(2 * BW + 1):
        inside = (abs(offset - BW) <= band_width).astype(jnp.float32)
        weight = inside[:, None] * band[:, offset, :].astype(jnp.float32)
        banded += weight[:, None] * padded[:, :, offset : offset + slab].astype(jnp.float32)

    image, part = pl.pallas_call(
        image_kernel,
        out_shape=(
            jax.ShapeDtypeStruct(by_slot.shape, jnp.bfloat16),
            jax.ShapeDtypeStruct((vecs // 2, 2 * vecs), jnp.float32),
        ),
        in_specs=[SMEM] * 4 + [VMEM] * 5,
        out_specs=(VMEM, VMEM),
        scratch_shapes=[pltpu.VMEM(by_slot.shape, jnp.float32)],
        compiler_params=PARAMS,
        name="image",
    )(slot, group, target_local, live, relayed, straight, coupling, banded, by_slot)
    piece = scatter(part, ("x", "core"))
    piece = jnp.sum(exchange(piece, ("y", "rad")), axis=0)
    projected = gather(piece, ("x", "core"))
    residual, rayleigh = pl.pallas_call(
        residual_kernel,
        out_shape=(
            jax.ShapeDtypeStruct(by_slot.shape, jnp.bfloat16),
            jax.ShapeDtypeStruct((vecs, vecs), jnp.float32),
        ),
        in_specs=[VMEM] * 4,
        out_specs=(VMEM, VMEM),
        compiler_params=PARAMS,
        name="residual",
    )(inverse, projected, by_slot, image)
    return jnp.transpose(residual, (1, 0, 2)), rayleigh


def solution(mesh):
    chan, rad = mesh.shape["chan"], mesh.shape["rad"]
    fine = Mesh(
        mesh.devices.reshape(chan // (X_CHIPS * CORES), X_CHIPS, CORES, rad),
        ("y", "x", "core", "rad"),
    )
    placed = (
        P(None, CHAN, "rad"),
        P(CHAN, None, "rad"),
        P(CHAN),
        P(CHAN),
        P(CHAN, "rad", None),
        P(CHAN),
        P(CHAN),
        P(CHAN),
        P(),
    )
    return jax.shard_map(
        body, mesh=fine, in_specs=placed, out_specs=(P(None, CHAN, "rad"), P()), check_vma=False
    )
```

```python
import functools

import jax
import jax.numpy as jnp
from jax import lax
from jax.experimental import pallas as pl
from jax.experimental.pallas import tpu as pltpu
from jax.sharding import Mesh, PartitionSpec as P

BW = 8
BLK = 256
CORES = 2
X_CHIPS = 4
UNROLL = 8
INNER = ("x", "core")
CHAN = ("y", "x", "core")
VMEM = pl.BlockSpec(memory_space=pltpu.VMEM)
SMEM = pl.BlockSpec(memory_space=pltpu.SMEM)
NT = (((1,), (1,)), ((), ()))
HIGH = lax.Precision.HIGHEST
PARAMS = pltpu.CompilerParams(vmem_limit_bytes=40 * 1024 * 1024)


def pack(square):
    half = square.shape[0] // 2
    return jnp.concatenate([square[:half], square[half:]], axis=1)


def unpack(packed):
    half = packed.shape[1] // 2
    return jnp.concatenate([packed[:, :half], packed[:, half:]], axis=0)


def gram_of(rows):
    acc = None
    for c in range(rows.shape[0]):
        term = lax.dot_general(rows[c], rows[c], NT, preferred_element_type=jnp.float32)
        acc = term if acc is None else acc + term
    return acc


def pick_kernel(per_group, want, rows, out, gram):
    @pl.loop(0, out.shape[0])
    def _(i):
        group = lax.rem(i, rows.shape[0] // per_group)
        out[i] = rows[group * per_group + want[i]]

    gram[...] = pack(gram_of(rows))


def image_kernel(slot, target, live, rows, coupling, banded, trial, gram, image, sent, total):
    total[...] = banded[...]

    @pl.loop(0, coupling.shape[0], step=UNROLL)
    def _(first):
        for i in range(UNROLL):
            p = first + i
            part = lax.dot_general(
                rows[slot[p]], coupling[p], NT, preferred_element_type=jnp.float32
            )
            total[target[p]] += part * live[p]

    acc = jnp.zeros((trial.shape[1], trial.shape[1]), jnp.float32)
    for c in range(total.shape[0]):
        rounded = total[c].astype(jnp.bfloat16)
        image[c] = rounded
        acc += lax.dot_general(trial[c], rounded, NT, preferred_element_type=jnp.float32)
    packed = pack(acc)
    summed = jnp.sum(gram[...], axis=0)
    piece = sent.shape[1] - summed.shape[0]
    for j in range(sent.shape[0]):
        sent[j, :piece] = packed[j * piece : (j + 1) * piece]
        sent[j, piece:] = summed


def middle_kernel(received, spread, gram):
    whole = jnp.sum(received[...], axis=0)
    piece = spread.shape[1]
    for j in range(spread.shape[0]):
        spread[j] = whole[:piece]
    gram[...] = unpack(whole[piece:])


def spread_kernel(received, spread):
    whole = jnp.sum(received[...], axis=0)
    for j in range(spread.shape[0]):
        spread[j] = whole


def residual_kernel(inverse, projected, trial, image, residual, rayleigh):
    inv = inverse[...]
    half = jnp.dot(inv, unpack(projected[...]), precision=HIGH, preferred_element_type=jnp.float32)
    full = lax.dot_general(
        inv, half, (((0,), (0,)), ((), ())), precision=HIGH, preferred_element_type=jnp.float32
    )
    rayleigh[...] = full
    flipped = full.T.astype(jnp.bfloat16)
    for c in range(trial.shape[0]):
        fit = jnp.dot(flipped, trial[c], preferred_element_type=jnp.float32)
        residual[c] = (image[c].astype(jnp.float32) - fit).astype(jnp.bfloat16)


def call(kernel, name, shapes, specs, *operands, scratch=()):
    several = isinstance(shapes, tuple)
    return pl.pallas_call(
        kernel,
        out_shape=shapes,
        in_specs=specs,
        out_specs=(VMEM,) * len(shapes) if several else VMEM,
        scratch_shapes=scratch,
        compiler_params=PARAMS,
        name=name,
    )(*operands)


def f32(*shape):
    return jax.ShapeDtypeStruct(shape, jnp.float32)


def bf16(*shape):
    return jax.ShapeDtypeStruct(shape, jnp.bfloat16)


def lookup(table, wanted_ids):
    match = wanted_ids[:, None] == jnp.arange(table.shape[0], dtype=jnp.int32)[None, :]
    return jnp.sum(jnp.where(match, table[None, :], 0), axis=1)


def body(trial, band, band_width, energies, coupling, reach, pair_target, pair_source, chan_slot):
    vecs, slots, slab = trial.shape
    ys, xs, cores, slabs = (lax.axis_size(a) for a in ("y", "x", "core", "rad"))
    me = (lax.axis_index("y") * xs + lax.axis_index("x")) * cores + lax.axis_index("core")
    columns = xs * cores

    source_slot = lookup(chan_slot, pair_source)
    target_local = lookup(chan_slot, pair_target) - me * slots
    group = source_slot // slots
    member = source_slot - group * slots
    hit = group[:, None] == jnp.arange(ys * columns, dtype=jnp.int32)[None, :]
    need = jnp.sum(jnp.where(hit, member[:, None], 0), axis=0)
    want = lax.all_to_all(need.reshape(ys, columns).T, INNER, 0, 0, tiled=True)
    slot = lax.rem(group, columns) * ys + group // columns
    live = (lax.axis_index("rad") < reach).astype(jnp.float32)

    by_slot = jnp.transpose(trial, (1, 0, 2))
    column = lax.all_gather(by_slot, "y", axis=0, tiled=True)
    picked, gram = call(
        functools.partial(pick_kernel, slots),
        "pick",
        (bf16(columns * ys, vecs, slab), f32(vecs // 2, 2 * vecs)),
        [SMEM, VMEM],
        want.reshape(-1),
        column,
    )
    rows = lax.all_to_all(picked, INNER, 0, 0, tiled=True)
    gram = lax.all_gather(gram, "rad")

    up = [(i, i + 1) for i in range(slabs - 1)]
    before = lax.ppermute(by_slot[:, :, slab - BW :], "rad", up)
    after = lax.ppermute(by_slot[:, :, :BW], "rad", [(j, i) for i, j in up])
    padded = jnp.concatenate([before, by_slot, after], axis=2)
    banded = energies[:, None, None] * by_slot.astype(jnp.float32)
    for offset in range(2 * BW + 1):
        inside = (abs(offset - BW) <= band_width).astype(jnp.float32)
        weight = inside[:, None] * band[:, offset, :].astype(jnp.float32)
        banded += weight[:, None] * padded[:, :, offset : offset + slab].astype(jnp.float32)

    half = vecs // 2
    piece = half // columns
    image, sent = call(
        image_kernel,
        "image",
        (bf16(*by_slot.shape), f32(columns, piece + half, 2 * vecs)),
        [SMEM] * 3 + [VMEM] * 5,
        slot,
        target_local,
        live,
        rows,
        coupling,
        banded,
        by_slot,
        gram,
        scratch=[pltpu.VMEM(by_slot.shape, jnp.float32)],
    )
    received = lax.all_to_all(sent, INNER, 0, 0, tiled=True)
    spread, gram = call(
        middle_kernel, "middle", (f32(ys * slabs, piece, 2 * vecs), f32(vecs, vecs)), [VMEM], received
    )
    received = lax.all_to_all(spread, ("y", "rad"), 0, 0, tiled=True)
    factor = jnp.linalg.cholesky(gram)
    inverse = lax.linalg.triangular_solve(
        factor, jnp.eye(vecs, dtype=jnp.float32), left_side=True, lower=True
    )
    spread = call(spread_kernel, "spread", f32(columns, piece, 2 * vecs), [VMEM], received)
    projected = lax.all_to_all(spread, INNER, 0, 0, tiled=True).reshape(half, 2 * vecs)
    residual, rayleigh = call(
        residual_kernel,
        "residual",
        (bf16(*by_slot.shape), f32(vecs, vecs)),
        [VMEM] * 4,
        inverse,
        projected,
        by_slot,
        image,
    )
    return jnp.transpose(residual, (1, 0, 2)), rayleigh


def solution(mesh):
    chan, rad = mesh.shape["chan"], mesh.shape["rad"]
    fine = Mesh(
        mesh.devices.reshape(chan // (X_CHIPS * CORES), X_CHIPS, CORES, rad),
        ("y", "x", "core", "rad"),
    )
    placed = (
        P(None, CHAN, "rad"),
        P(CHAN, None, "rad"),
        P(CHAN),
        P(CHAN),
        P(CHAN, "rad", None),
        P(CHAN),
        P(CHAN),
        P(CHAN),
        P(),
    )
    return jax.shard_map(
        body, mesh=fine, in_specs=placed, out_specs=(P(None, CHAN, "rad"), P()), check_vma=False
    )
```

```python
import functools

import jax
import jax.numpy as jnp
from jax import lax
from jax.experimental import pallas as pl
from jax.experimental.pallas import tpu as pltpu
from jax.sharding import Mesh, PartitionSpec as P

BW = 8
BLK = 256
CORES = 2
X_CHIPS = 4
UNROLL = 8
INNER = ("x", "core")
CHAN = ("y", "x", "core")
VMEM = pl.BlockSpec(memory_space=pltpu.VMEM)
ANY = pl.BlockSpec(memory_space=pl.ANY)
SMEM = pl.BlockSpec(memory_space=pltpu.SMEM)
NT = (((1,), (1,)), ((), ()))
HIGH = lax.Precision.HIGHEST
MIB = 1024 * 1024


def pack(square):
    half = square.shape[0] // 2
    return jnp.concatenate([square[:half], square[half:]], axis=1)


def unpack(packed):
    half = packed.shape[1] // 2
    return jnp.concatenate([packed[:, :half], packed[:, half:]], axis=0)


def gram_of(rows):
    acc = None
    for c in range(rows.shape[0]):
        term = lax.dot_general(rows[c], rows[c], NT, preferred_element_type=jnp.float32)
        acc = term if acc is None else acc + term
    return acc


def pick_kernel(mine, need, rows, out, sems):
    receivers = need.shape[0]
    groups = out.shape[0] // receivers
    per_group = rows.shape[0] // groups
    columns = need.shape[1] // groups

    def copy(i):
        receiver, group = lax.div(i, groups), lax.rem(i, groups)
        chosen = group * per_group + need[receiver, group * columns + mine[0]]
        return pltpu.make_async_copy(rows.at[chosen], out.at[i], sems.at[i])

    @pl.loop(0, out.shape[0])
    def _(i):
        copy(i).start()

    @pl.loop(0, out.shape[0])
    def _(i):
        copy(i).wait()


def gram_kernel(rows, gram):
    gram[...] = pack(gram_of(rows))


def inverse_kernel(square, inverse):
    size = square.shape[0]
    down = lax.broadcasted_iota(jnp.int32, (size, size), 0)
    across = lax.broadcasted_iota(jnp.int32, (size, size), 1)
    value = square[...]
    for k in range(size):
        scale = 1.0 / value[k : k + 1, k : k + 1]
        row = jnp.where(across[:1] == k, 1.0, value[k : k + 1]) * scale
        column = jnp.where(down[:, :1] == k, -1.0, value[:, k : k + 1])
        rest = jnp.where((down == k) | (across == k), 0.0, value)
        value = rest - column * row
    inverse[...] = value


def image_kernel(slot, target, live, rows, coupling, banded, trial, gram, image, sent, total, held, sems):
    def copy(p):
        return pltpu.make_async_copy(coupling.at[p], held.at[p], sems.at[p])

    @pl.loop(0, coupling.shape[0])
    def _(p):
        copy(p).start()

    total[...] = banded[...]

    @pl.loop(0, coupling.shape[0], step=UNROLL)
    def _(first):
        for i in range(UNROLL):
            copy(first + i).wait()
        for i in range(UNROLL):
            p = first + i
            part = lax.dot_general(
                rows[slot[p]], held[p], NT, preferred_element_type=jnp.float32
            )
            total[target[p]] += part * live[p]

    acc = jnp.zeros((trial.shape[1], trial.shape[1]), jnp.float32)
    for c in range(total.shape[0]):
        rounded = total[c].astype(jnp.bfloat16)
        image[c] = rounded
        acc += lax.dot_general(trial[c], rounded, NT, preferred_element_type=jnp.float32)
    packed = pack(acc)
    summed = jnp.sum(gram[...], axis=0)
    piece = sent.shape[1] - summed.shape[0]
    for j in range(sent.shape[0]):
        sent[j, :piece] = packed[j * piece : (j + 1) * piece]
        sent[j, piece:] = summed


def middle_kernel(received, spread, gram):
    whole = jnp.sum(received[...], axis=0)
    piece = spread.shape[1]
    for j in range(spread.shape[0]):
        spread[j] = whole[:piece]
    gram[...] = unpack(whole[piece:])


def spread_kernel(received, spread):
    whole = jnp.sum(received[...], axis=0)
    for j in range(spread.shape[0]):
        spread[j] = whole


def residual_kernel(inverse, projected, trial, image, residual, rayleigh):
    full = jnp.dot(
        inverse[...],
        unpack(projected[...]),
        precision=HIGH,
        preferred_element_type=jnp.float32,
    )
    rayleigh[...] = full
    flipped = full.T.astype(jnp.bfloat16)
    for c in range(trial.shape[0]):
        fit = jnp.dot(flipped, trial[c], preferred_element_type=jnp.float32)
        residual[c] = (image[c].astype(jnp.float32) - fit).astype(jnp.bfloat16)


def call(kernel, name, shapes, specs, *operands, out=VMEM, scratch=(), limit=40):
    several = isinstance(shapes, tuple)
    return pl.pallas_call(
        kernel,
        out_shape=shapes,
        in_specs=specs,
        out_specs=(VMEM,) * len(shapes) if several else out,
        scratch_shapes=scratch,
        compiler_params=pltpu.CompilerParams(vmem_limit_bytes=limit * MIB),
        name=name,
    )(*operands)


def f32(*shape):
    return jax.ShapeDtypeStruct(shape, jnp.float32)


def bf16(*shape):
    return jax.ShapeDtypeStruct(shape, jnp.bfloat16)


def lookup(table, wanted_ids):
    match = wanted_ids[:, None] == jnp.arange(table.shape[0], dtype=jnp.int32)[None, :]
    return jnp.sum(jnp.where(match, table[None, :], 0), axis=1)


def body(trial, band, band_width, energies, coupling, reach, pair_target, pair_source, chan_slot):
    vecs, slots, slab = trial.shape
    ys, xs, cores, slabs = (lax.axis_size(a) for a in ("y", "x", "core", "rad"))
    me = (lax.axis_index("y") * xs + lax.axis_index("x")) * cores + lax.axis_index("core")
    columns = xs * cores

    source_slot = lookup(chan_slot, pair_source)
    target_local = lookup(chan_slot, pair_target) - me * slots
    group = source_slot // slots
    member = source_slot - group * slots
    hit = group[:, None] == jnp.arange(ys * columns, dtype=jnp.int32)[None, :]
    need = jnp.sum(jnp.where(hit, member[:, None], 0), axis=0)
    needed = lax.all_gather(need, INNER)
    slot = lax.rem(group, columns) * ys + group // columns
    live = (lax.axis_index("rad") < reach).astype(jnp.float32)

    by_slot = jnp.transpose(trial, (1, 0, 2))
    column = lax.all_to_all(
        jnp.broadcast_to(by_slot[None], (ys,) + by_slot.shape), "y", 0, 0, tiled=True
    ).reshape(ys * slots, vecs, slab)

    up = [(i, i + 1) for i in range(slabs - 1)]
    before = lax.ppermute(by_slot[:, :, slab - BW :], "rad", up)
    after = lax.ppermute(by_slot[:, :, :BW], "rad", [(j, i) for i, j in up])
    padded = jnp.concatenate([before, by_slot, after], axis=2)
    banded = energies[:, None, None] * by_slot.astype(jnp.float32)
    for offset in range(2 * BW + 1):
        inside = (abs(offset - BW) <= band_width).astype(jnp.float32)
        weight = inside[:, None] * band[:, offset, :].astype(jnp.float32)
        banded += weight[:, None] * padded[:, :, offset : offset + slab].astype(jnp.float32)

    column, banded = lax.optimization_barrier((column, banded))
    mine = (lax.axis_index("x") * cores + lax.axis_index("core")).reshape(1)
    picked = call(
        pick_kernel,
        "pick",
        bf16(columns * ys, vecs, slab),
        [SMEM, SMEM, ANY],
        mine,
        needed,
        column,
        out=ANY,
        scratch=[pltpu.SemaphoreType.DMA((columns * ys,))],
    )
    column, picked = lax.optimization_barrier((column, picked))
    rows = lax.all_to_all(picked, INNER, 0, 0, tiled=True)
    gram = lax.all_gather(call(gram_kernel, "gram", f32(vecs // 2, 2 * vecs), [VMEM], column), "rad")

    half = vecs // 2
    piece = half // columns
    image, sent = call(
        image_kernel,
        "image",
        (bf16(*by_slot.shape), f32(columns, piece + half, 2 * vecs)),
        [SMEM] * 3 + [VMEM, ANY] + [VMEM] * 3,
        slot,
        target_local,
        live,
        rows,
        coupling,
        banded,
        by_slot,
        gram,
        scratch=[
            pltpu.VMEM(by_slot.shape, jnp.float32),
            pltpu.VMEM(coupling.shape, jnp.bfloat16),
            pltpu.SemaphoreType.DMA(coupling.shape[:1]),
        ],
        limit=50,
    )
    received = lax.all_to_all(sent, INNER, 0, 0, tiled=True)
    spread, gram = call(
        middle_kernel, "middle", (f32(ys * slabs, piece, 2 * vecs), f32(vecs, vecs)), [VMEM], received
    )
    received = lax.all_to_all(spread, ("y", "rad"), 0, 0, tiled=True)
    inverse = call(inverse_kernel, "inverse", f32(vecs, vecs), [VMEM], gram)
    spread = call(spread_kernel, "spread", f32(columns, piece, 2 * vecs), [VMEM], received)
    projected = lax.all_to_all(spread, INNER, 0, 0, tiled=True).reshape(half, 2 * vecs)
    residual, rayleigh = call(
        residual_kernel,
        "residual",
        (bf16(*by_slot.shape), f32(vecs, vecs)),
        [VMEM] * 4,
        inverse,
        projected,
        by_slot,
        image,
    )
    return jnp.transpose(residual, (1, 0, 2)), rayleigh


def solution(mesh):
    chan, rad = mesh.shape["chan"], mesh.shape["rad"]
    fine = Mesh(
        mesh.devices.reshape(chan // (X_CHIPS * CORES), X_CHIPS, CORES, rad),
        ("y", "x", "core", "rad"),
    )
    placed = (
        P(None, CHAN, "rad"),
        P(CHAN, None, "rad"),
        P(CHAN),
        P(CHAN),
        P(CHAN, "rad", None),
        P(CHAN),
        P(CHAN),
        P(CHAN),
        P(),
    )
    return jax.shard_map(
        body, mesh=fine, in_specs=placed, out_specs=(P(None, CHAN, "rad"), P()), check_vma=False
    )
```

```python
import functools

import jax
import jax.numpy as jnp
from jax import lax
from jax.experimental import pallas as pl
from jax.experimental.pallas import tpu as pltpu
from jax.sharding import Mesh, PartitionSpec as P

BW = 8
BLK = 256
CORES = 2
X_CHIPS = 4
CHUNK = 8
INNER = ("x", "core")
CHAN = ("y", "x", "core")
VMEM = pl.BlockSpec(memory_space=pltpu.VMEM)
ANY = pl.BlockSpec(memory_space=pl.ANY)
SMEM = pl.BlockSpec(memory_space=pltpu.SMEM)
NT = (((1,), (1,)), ((), ()))
HIGH = lax.Precision.HIGHEST
MIB = 1024 * 1024


def pack(square):
    half = square.shape[0] // 2
    return jnp.concatenate([square[:half], square[half:]], axis=1)


def unpack(packed):
    half = packed.shape[1] // 2
    return jnp.concatenate([packed[:, :half], packed[:, half:]], axis=0)


def gram_of(rows):
    acc = None
    for c in range(rows.shape[0]):
        term = lax.dot_general(rows[c], rows[c], NT, preferred_element_type=jnp.float32)
        acc = term if acc is None else acc + term
    return acc


def pick_kernel(mine, need, rows, out):
    receivers = need.shape[0]
    groups = out.shape[0] // receivers
    per_group = rows.shape[0] // groups
    columns = need.shape[1] // groups

    @pl.loop(0, receivers)
    def _(receiver):
        for group in range(groups):
            chosen = group * per_group + need[receiver, group * columns + mine[0]]
            out[receiver * groups + group] = rows[chosen]


def gram_kernel(rows, gram):
    gram[...] = pack(gram_of(rows))


def inverse_kernel(square, inverse):
    size = square.shape[0]
    down = lax.broadcasted_iota(jnp.int32, (size, size), 0)
    across = lax.broadcasted_iota(jnp.int32, (size, size), 1)
    value = square[...]
    for k in range(size):
        scale = 1.0 / value[k : k + 1, k : k + 1]
        row = jnp.where(across[:1] == k, 1.0, value[k : k + 1]) * scale
        column = jnp.where(down[:, :1] == k, -1.0, value[:, k : k + 1])
        rest = jnp.where((down == k) | (across == k), 0.0, value)
        value = rest - column * row
    inverse[...] = value


def image_kernel(
    slot, target, live, rows, coupling, banded, trial, image, sent, total, held, sems
):
    def copy(chunk):
        part = pl.ds(chunk * CHUNK, CHUNK)
        return pltpu.make_async_copy(coupling.at[part], held.at[part], sems.at[chunk])

    for chunk in range(sems.shape[0]):
        copy(chunk).start()
    total[...] = banded[...]

    @pl.loop(0, sems.shape[0])
    def _(chunk):
        copy(chunk).wait()
        for i in range(CHUNK):
            p = chunk * CHUNK + i
            part = lax.dot_general(
                rows[slot[p]], held[p], NT, preferred_element_type=jnp.float32
            )
            total[target[p]] += part * live[p]

    acc = jnp.zeros((trial.shape[1], trial.shape[1]), jnp.float32)
    for c in range(total.shape[0]):
        rounded = total[c].astype(jnp.bfloat16)
        image[c] = rounded
        acc += lax.dot_general(trial[c], rounded, NT, preferred_element_type=jnp.float32)
    sent[...] = pack(acc)


def middle_kernel(received, gram, spread):
    whole = jnp.concatenate([gram[...], jnp.sum(received[...], axis=0)], axis=0)
    for j in range(spread.shape[0]):
        spread[j] = whole


def last_kernel(received, spread, gram):
    piece = spread.shape[1]
    part = received.shape[1] - piece
    count = gram.shape[0] // 2 // part
    over_x = received.shape[0] // count
    found = []
    for y in range(count):
        found.append(jnp.sum(received[y * over_x : (y + 1) * over_x], axis=0))
    whole = found[0][part:]
    for y in range(1, count):
        whole += found[y][part:]
    for j in range(spread.shape[0]):
        spread[j] = whole
    gram[...] = unpack(jnp.concatenate([f[:part] for f in found], axis=0))


def residual_kernel(inverse, projected, trial, image, residual, rayleigh):
    full = jnp.dot(
        inverse[...],
        unpack(projected[...]),
        precision=HIGH,
        preferred_element_type=jnp.float32,
    )
    rayleigh[...] = full
    flipped = full.T.astype(jnp.bfloat16)
    for c in range(trial.shape[0]):
        fit = jnp.dot(flipped, trial[c], preferred_element_type=jnp.float32)
        residual[c] = (image[c].astype(jnp.float32) - fit).astype(jnp.bfloat16)


def call(kernel, name, shapes, specs, *operands, scratch=(), limit=40):
    several = isinstance(shapes, tuple)
    return pl.pallas_call(
        kernel,
        out_shape=shapes,
        in_specs=specs,
        out_specs=(VMEM,) * len(shapes) if several else VMEM,
        scratch_shapes=scratch,
        compiler_params=pltpu.CompilerParams(vmem_limit_bytes=limit * MIB),
        name=name,
    )(*operands)


def f32(*shape):
    return jax.ShapeDtypeStruct(shape, jnp.float32)


def bf16(*shape):
    return jax.ShapeDtypeStruct(shape, jnp.bfloat16)


def lookup(table, wanted_ids):
    match = wanted_ids[:, None] == jnp.arange(table.shape[0], dtype=jnp.int32)[None, :]
    return jnp.sum(jnp.where(match, table[None, :], 0), axis=1)


def body(trial, band, band_width, energies, coupling, reach, pair_target, pair_source, chan_slot):
    vecs, slots, slab = trial.shape
    ys, xs, cores, slabs = (lax.axis_size(a) for a in ("y", "x", "core", "rad"))
    me = (lax.axis_index("y") * xs + lax.axis_index("x")) * cores + lax.axis_index("core")
    columns = xs * cores

    source_slot = lookup(chan_slot, pair_source)
    target_local = lookup(chan_slot, pair_target) - me * slots
    group = source_slot // slots
    member = source_slot - group * slots
    hit = group[:, None] == jnp.arange(ys * columns, dtype=jnp.int32)[None, :]
    need = jnp.sum(jnp.where(hit, member[:, None], 0), axis=0)
    needed = lax.all_gather(need, INNER)
    slot = lax.rem(group, columns) * ys + group // columns

    by_slot = jnp.transpose(trial, (1, 0, 2))
    column = lax.all_to_all(
        jnp.broadcast_to(by_slot[None], (ys,) + by_slot.shape), "y", 0, 0, tiled=True
    ).reshape(ys * slots, vecs, slab)

    up = [(i, i + 1) for i in range(slabs - 1)]
    before = lax.ppermute(by_slot[:, :, slab - BW :], "rad", up)
    after = lax.ppermute(by_slot[:, :, :BW], "rad", [(j, i) for i, j in up])
    padded = jnp.concatenate([before, by_slot, after], axis=2)
    banded = energies[:, None, None] * by_slot.astype(jnp.float32)
    for offset in range(2 * BW + 1):
        inside = (abs(offset - BW) <= band_width).astype(jnp.float32)
        weight = inside[:, None] * band[:, offset, :].astype(jnp.float32)
        banded += weight[:, None] * padded[:, :, offset : offset + slab].astype(jnp.float32)

    column, banded = lax.optimization_barrier((column, banded))
    mine = (lax.axis_index("x") * cores + lax.axis_index("core")).reshape(1)
    picked = call(
        pick_kernel, "pick", bf16(columns * ys, vecs, slab), [SMEM, SMEM, VMEM], mine, needed, column
    )
    column, picked = lax.optimization_barrier((column, picked))
    rows = lax.all_to_all(picked, INNER, 0, 0, tiled=True)
    half = vecs // 2
    gram = call(gram_kernel, "gram", f32(half, 2 * vecs), [VMEM], column)
    gram = lax.dynamic_slice_in_dim(gram, lax.axis_index("y") * (half // ys), half // ys)
    gram = lax.psum(lax.psum(gram, "core"), "rad")
    rows, gram = lax.optimization_barrier((rows, gram))

    image, sent = call(
        image_kernel,
        "image",
        (bf16(*by_slot.shape), f32(half, 2 * vecs)),
        [SMEM] * 3 + [VMEM, ANY] + [VMEM] * 2,
        slot,
        target_local,
        (lax.axis_index("rad") < reach).astype(jnp.float32),
        rows,
        coupling,
        banded,
        by_slot,
        scratch=[
            pltpu.VMEM(by_slot.shape, jnp.float32),
            pltpu.VMEM(coupling.shape, jnp.bfloat16),
            pltpu.SemaphoreType.DMA((coupling.shape[0] // CHUNK,)),
        ],
        limit=50,
    )
    shared = cores * slabs
    piece = half // shared
    sent = sent.reshape(shared, piece, 2 * vecs)
    received = lax.all_to_all(sent, ("core", "rad"), 0, 0, tiled=True)
    spread = call(
        middle_kernel,
        "middle",
        f32(ys * xs, half // ys + piece, 2 * vecs),
        [VMEM, VMEM],
        received,
        gram,
    )
    received = lax.all_to_all(spread, ("y", "x"), 0, 0, tiled=True)
    spread, gram = call(
        last_kernel, "last", (f32(shared, piece, 2 * vecs), f32(vecs, vecs)), [VMEM], received
    )
    inverse = call(inverse_kernel, "inverse", f32(vecs, vecs), [VMEM], gram)
    projected = lax.all_to_all(spread, ("core", "rad"), 0, 0, tiled=True).reshape(half, 2 * vecs)
    residual, rayleigh = call(
        residual_kernel,
        "residual",
        (bf16(*by_slot.shape), f32(vecs, vecs)),
        [VMEM] * 4,
        inverse,
        projected,
        by_slot,
        image,
    )
    return jnp.transpose(residual, (1, 0, 2)), rayleigh


def solution(mesh):
    chan, rad = mesh.shape["chan"], mesh.shape["rad"]
    fine = Mesh(
        mesh.devices.reshape(chan // (X_CHIPS * CORES), X_CHIPS, CORES, rad),
        ("y", "x", "core", "rad"),
    )
    placed = (
        P(None, CHAN, "rad"),
        P(CHAN, None, "rad"),
        P(CHAN),
        P(CHAN),
        P(CHAN, "rad", None),
        P(CHAN),
        P(CHAN),
        P(CHAN),
        P(),
    )
    return jax.shard_map(
        body, mesh=fine, in_specs=placed, out_specs=(P(None, CHAN, "rad"), P()), check_vma=False
    )
```

```python
import functools

import jax
import jax.numpy as jnp
from jax import lax
from jax.experimental import pallas as pl
from jax.experimental.pallas import tpu as pltpu
from jax.sharding import Mesh, PartitionSpec as P

BW = 8
BLK = 256
CORES = 2
X_CHIPS = 4
CHUNK = 4
INNER = ("x", "core")
CHAN = ("y", "x", "core")
VMEM = pl.BlockSpec(memory_space=pltpu.VMEM)
ANY = pl.BlockSpec(memory_space=pl.ANY)
SMEM = pl.BlockSpec(memory_space=pltpu.SMEM)
NT = (((1,), (1,)), ((), ()))
HIGH = lax.Precision.HIGHEST
MIB = 1024 * 1024


def pack(square):
    half = square.shape[0] // 2
    return jnp.concatenate([square[:half], square[half:]], axis=1)


def unpack(packed):
    half = packed.shape[1] // 2
    return jnp.concatenate([packed[:, :half], packed[:, half:]], axis=0)


def gram_of(rows):
    acc = None
    for c in range(rows.shape[0]):
        term = lax.dot_general(rows[c], rows[c], NT, preferred_element_type=jnp.float32)
        acc = term if acc is None else acc + term
    return acc


def pick_kernel(mine, need, *refs):
    *parts, out, rows = refs
    count = len(parts)
    for s, part in enumerate(parts):
        rows[lax.rem(mine[1] - s + count, count)] = part[...]
    receivers = need.shape[0]
    columns = need.shape[1] // count

    @pl.loop(0, receivers)
    def _(receiver):
        for group in range(count):
            chosen = need[receiver, group * columns + mine[0]]
            out[receiver * count + group] = rows[group, chosen]


def gram_kernel(*refs):
    *parts, gram = refs
    acc = gram_of(parts[0])
    for part in parts[1:]:
        acc += gram_of(part)
    gram[...] = pack(acc)


def inverse_kernel(square, inverse):
    size = square.shape[0]
    down = lax.broadcasted_iota(jnp.int32, (size, size), 0)
    across = lax.broadcasted_iota(jnp.int32, (size, size), 1)
    value = square[...]
    for k in range(size):
        scale = 1.0 / value[k : k + 1, k : k + 1]
        row = jnp.where(across[:1] == k, 1.0, value[k : k + 1]) * scale
        column = jnp.where(down[:, :1] == k, -1.0, value[:, k : k + 1])
        rest = jnp.where((down == k) | (across == k), 0.0, value)
        value = rest - column * row
    inverse[...] = value


def image_kernel(
    slot, target, live, rows, coupling, banded, trial, image, sent, total, held, sems
):
    def copy(chunk):
        part = pl.ds(chunk * CHUNK, CHUNK)
        return pltpu.make_async_copy(coupling.at[part], held.at[part], sems.at[chunk])

    for chunk in range(sems.shape[0]):
        copy(chunk).start()
    total[...] = banded[...]

    @pl.loop(0, sems.shape[0])
    def _(chunk):
        copy(chunk).wait()
        for i in range(CHUNK):
            p = chunk * CHUNK + i
            part = lax.dot_general(
                rows[slot[p]], held[p], NT, preferred_element_type=jnp.float32
            )
            total[target[p]] += part * live[p]

    acc = jnp.zeros((trial.shape[1], trial.shape[1]), jnp.float32)
    for c in range(total.shape[0]):
        rounded = total[c].astype(jnp.bfloat16)
        image[c] = rounded
        acc += lax.dot_general(trial[c], rounded, NT, preferred_element_type=jnp.float32)
    sent[...] = pack(acc)


def middle_kernel(received, gram, spread):
    whole = jnp.concatenate([gram[...], jnp.sum(received[...], axis=0)], axis=0)
    for j in range(spread.shape[0]):
        spread[j] = whole


def last_kernel(received, spread, gram):
    piece = spread.shape[1]
    part = received.shape[1] - piece
    count = gram.shape[0] // 2 // part
    over_x = received.shape[0] // count
    found = []
    for y in range(count):
        found.append(jnp.sum(received[y * over_x : (y + 1) * over_x], axis=0))
    whole = found[0][part:]
    for y in range(1, count):
        whole += found[y][part:]
    for j in range(spread.shape[0]):
        spread[j] = whole
    gram[...] = unpack(jnp.concatenate([f[:part] for f in found], axis=0))


def residual_kernel(inverse, projected, trial, image, residual, rayleigh):
    full = jnp.dot(
        inverse[...],
        unpack(projected[...]),
        precision=HIGH,
        preferred_element_type=jnp.float32,
    )
    rayleigh[...] = full
    flipped = full.T.astype(jnp.bfloat16)
    for c in range(trial.shape[0]):
        fit = jnp.dot(flipped, trial[c], preferred_element_type=jnp.float32)
        residual[c] = (image[c].astype(jnp.float32) - fit).astype(jnp.bfloat16)


def call(kernel, name, shapes, specs, *operands, scratch=(), limit=40):
    several = isinstance(shapes, tuple)
    return pl.pallas_call(
        kernel,
        out_shape=shapes,
        in_specs=specs,
        out_specs=(VMEM,) * len(shapes) if several else VMEM,
        scratch_shapes=scratch,
        compiler_params=pltpu.CompilerParams(vmem_limit_bytes=limit * MIB),
        name=name,
    )(*operands)


def f32(*shape):
    return jax.ShapeDtypeStruct(shape, jnp.float32)


def bf16(*shape):
    return jax.ShapeDtypeStruct(shape, jnp.bfloat16)


def lookup(table, wanted_ids):
    match = wanted_ids[:, None] == jnp.arange(table.shape[0], dtype=jnp.int32)[None, :]
    return jnp.sum(jnp.where(match, table[None, :], 0), axis=1)


def body(trial, band, band_width, energies, coupling, reach, pair_target, pair_source, chan_slot):
    vecs, slots, slab = trial.shape
    ys, xs, cores, slabs = (lax.axis_size(a) for a in ("y", "x", "core", "rad"))
    me = (lax.axis_index("y") * xs + lax.axis_index("x")) * cores + lax.axis_index("core")
    columns = xs * cores

    source_slot = lookup(chan_slot, pair_source)
    target_local = lookup(chan_slot, pair_target) - me * slots
    group = source_slot // slots
    member = source_slot - group * slots
    hit = group[:, None] == jnp.arange(ys * columns, dtype=jnp.int32)[None, :]
    need = jnp.sum(jnp.where(hit, member[:, None], 0), axis=0)
    needed = lax.all_gather(need, INNER)
    slot = lax.rem(group, columns) * ys + group // columns

    by_slot = jnp.transpose(trial, (1, 0, 2))
    column = [by_slot] * ys
    for s in sorted(range(1, ys), key=lambda s: min(s, ys - s), reverse=True):
        column[s] = lax.ppermute(by_slot, "y", [(i, (i + s) % ys) for i in range(ys)])

    up = [(i, i + 1) for i in range(slabs - 1)]
    before = lax.ppermute(by_slot[:, :, slab - BW :], "rad", up)
    after = lax.ppermute(by_slot[:, :, :BW], "rad", [(j, i) for i, j in up])
    padded = jnp.concatenate([before, by_slot, after], axis=2)
    banded = energies[:, None, None] * by_slot.astype(jnp.float32)
    for offset in range(2 * BW + 1):
        inside = (abs(offset - BW) <= band_width).astype(jnp.float32)
        weight = inside[:, None] * band[:, offset, :].astype(jnp.float32)
        banded += weight[:, None] * padded[:, :, offset : offset + slab].astype(jnp.float32)

    column, banded = lax.optimization_barrier((column, banded))
    mine = jnp.stack(
        [lax.axis_index("x") * cores + lax.axis_index("core"), lax.axis_index("y")]
    )
    picked = call(
        pick_kernel,
        "pick",
        bf16(columns * ys, vecs, slab),
        [SMEM, SMEM] + [VMEM] * ys,
        mine,
        needed,
        *column,
        scratch=[pltpu.VMEM((ys,) + by_slot.shape, jnp.bfloat16)],
    )
    column, picked = lax.optimization_barrier((column, picked))
    rows = lax.all_to_all(picked, INNER, 0, 0, tiled=True)
    half = vecs // 2
    gram = call(gram_kernel, "gram", f32(half, 2 * vecs), [VMEM] * ys, *column)
    gram = lax.dynamic_slice_in_dim(gram, lax.axis_index("y") * (half // ys), half // ys)
    gram = lax.psum(lax.psum(gram, "core"), "rad")
    rows, gram = lax.optimization_barrier((rows, gram))

    image, sent = call(
        image_kernel,
        "image",
        (bf16(*by_slot.shape), f32(half, 2 * vecs)),
        [SMEM] * 3 + [VMEM, ANY] + [VMEM] * 2,
        slot,
        target_local,
        (lax.axis_index("rad") < reach).astype(jnp.float32),
        rows,
        coupling,
        banded,
        by_slot,
        scratch=[
            pltpu.VMEM(by_slot.shape, jnp.float32),
            pltpu.VMEM(coupling.shape, jnp.bfloat16),
            pltpu.SemaphoreType.DMA((coupling.shape[0] // CHUNK,)),
        ],
        limit=50,
    )
    shared = cores * slabs
    piece = half // shared
    sent = sent.reshape(shared, piece, 2 * vecs)
    received = lax.all_to_all(sent, ("core", "rad"), 0, 0, tiled=True)
    spread = call(
        middle_kernel,
        "middle",
        f32(ys * xs, half // ys + piece, 2 * vecs),
        [VMEM, VMEM],
        received,
        gram,
    )
    received = lax.all_to_all(spread, ("y", "x"), 0, 0, tiled=True)
    spread, gram = call(
        last_kernel, "last", (f32(shared, piece, 2 * vecs), f32(vecs, vecs)), [VMEM], received
    )
    inverse = call(inverse_kernel, "inverse", f32(vecs, vecs), [VMEM], gram)
    projected = lax.all_to_all(spread, ("core", "rad"), 0, 0, tiled=True).reshape(half, 2 * vecs)
    residual, rayleigh = call(
        residual_kernel,
        "residual",
        (bf16(*by_slot.shape), f32(vecs, vecs)),
        [VMEM] * 4,
        inverse,
        projected,
        by_slot,
        image,
    )
    return jnp.transpose(residual, (1, 0, 2)), rayleigh


def solution(mesh):
    chan, rad = mesh.shape["chan"], mesh.shape["rad"]
    fine = Mesh(
        mesh.devices.reshape(chan // (X_CHIPS * CORES), X_CHIPS, CORES, rad),
        ("y", "x", "core", "rad"),
    )
    placed = (
        P(None, CHAN, "rad"),
        P(CHAN, None, "rad"),
        P(CHAN),
        P(CHAN),
        P(CHAN, "rad", None),
        P(CHAN),
        P(CHAN),
        P(CHAN),
        P(),
    )
    return jax.shard_map(
        body, mesh=fine, in_specs=placed, out_specs=(P(None, CHAN, "rad"), P()), check_vma=False
    )
```

```python
import functools

import jax
import jax.numpy as jnp
from jax import lax
from jax.experimental import pallas as pl
from jax.experimental.pallas import tpu as pltpu
from jax.sharding import Mesh, PartitionSpec as P

BW = 8
BLK = 256
CORES = 2
X_CHIPS = 4
CHUNK = 8
INNER = ("x", "core")
CHAN = ("y", "x", "core")
VMEM = pl.BlockSpec(memory_space=pltpu.VMEM)
ANY = pl.BlockSpec(memory_space=pl.ANY)
SMEM = pl.BlockSpec(memory_space=pltpu.SMEM)
NT = (((1,), (1,)), ((), ()))
HIGH = lax.Precision.HIGHEST
MIB = 1024 * 1024


def pack(square):
    half = square.shape[0] // 2
    return jnp.concatenate([square[:half], square[half:]], axis=1)


def unpack(packed):
    half = packed.shape[1] // 2
    return jnp.concatenate([packed[:, :half], packed[:, half:]], axis=0)


def gram_of(rows):
    acc = None
    for c in range(rows.shape[0]):
        term = lax.dot_general(rows[c], rows[c], NT, preferred_element_type=jnp.float32)
        acc = term if acc is None else acc + term
    return acc


def pick_kernel(mine, need, rows, out):
    receivers = need.shape[0]
    groups = out.shape[0] // receivers
    per_group = rows.shape[0] // groups
    columns = need.shape[1] // groups

    @pl.loop(0, receivers)
    def _(receiver):
        for group in range(groups):
            chosen = group * per_group + need[receiver, group * columns + mine[0]]
            out[receiver * groups + group] = rows[chosen]


def gram_kernel(rows, gram):
    gram[...] = pack(gram_of(rows))


def inverse_kernel(square, inverse):
    size = square.shape[0]
    down = lax.broadcasted_iota(jnp.int32, (size, size), 0)
    across = lax.broadcasted_iota(jnp.int32, (size, size), 1)
    value = square[...]
    for k in range(0, size, 2):
        at = [across[:1] == k, across[:1] == k + 1]
        first = 1.0 / value[k : k + 1, k : k + 1]
        beside = value[k : k + 1, k + 1 : k + 2]
        below = value[k + 1 : k + 2, k : k + 1] * first
        second = 1.0 / (value[k + 1 : k + 2, k + 1 : k + 2] - below * beside)
        top = jnp.where(at[0], 1.0, jnp.where(at[1], 0.0, value[k : k + 1]))
        low = jnp.where(at[0], 0.0, jnp.where(at[1], 1.0, value[k + 1 : k + 2]))
        low = (low - below * top) * second
        top = (top - beside * low) * first
        here = [down[:, :1] == k, down[:, :1] == k + 1]
        left = jnp.where(here[0], -1.0, jnp.where(here[1], 0.0, value[:, k : k + 1]))
        right = jnp.where(here[0], 0.0, jnp.where(here[1], -1.0, value[:, k + 1 : k + 2]))
        pivots = (down // 2 == k // 2) | (across // 2 == k // 2)
        value = jnp.where(pivots, 0.0, value) - left * top - right * low
    inverse[...] = value


def image_kernel(
    slot, target, live, rows, coupling, banded, trial, image, sent, total, held, sems
):
    def copy(chunk):
        part = pl.ds(chunk * CHUNK, CHUNK)
        return pltpu.make_async_copy(coupling.at[part], held.at[part], sems.at[chunk])

    for chunk in range(sems.shape[0]):
        copy(chunk).start()
    total[...] = banded[...]

    @pl.loop(0, sems.shape[0])
    def _(chunk):
        copy(chunk).wait()
        for i in range(CHUNK):
            p = chunk * CHUNK + i
            part = lax.dot_general(
                rows[slot[p]], held[p], NT, preferred_element_type=jnp.float32
            )
            total[target[p]] += part * live[p]

    acc = jnp.zeros((trial.shape[1], trial.shape[1]), jnp.float32)
    for c in range(total.shape[0]):
        rounded = total[c].astype(jnp.bfloat16)
        image[c] = rounded
        acc += lax.dot_general(trial[c], rounded, NT, preferred_element_type=jnp.float32)
    sent[...] = pack(acc)


def middle_kernel(received, gram, spread):
    whole = jnp.concatenate([gram[...], jnp.sum(received[...], axis=0)], axis=0)
    for j in range(spread.shape[0]):
        spread[j] = whole


def last_kernel(received, spread, gram):
    piece = spread.shape[1]
    part = received.shape[1] - piece
    count = gram.shape[0] // 2 // part
    over_x = received.shape[0] // count
    found = []
    for y in range(count):
        found.append(jnp.sum(received[y * over_x : (y + 1) * over_x], axis=0))
    whole = found[0][part:]
    for y in range(1, count):
        whole += found[y][part:]
    for j in range(spread.shape[0]):
        spread[j] = whole
    gram[...] = unpack(jnp.concatenate([f[:part] for f in found], axis=0))


def residual_kernel(inverse, projected, trial, image, residual, rayleigh):
    full = jnp.dot(
        inverse[...],
        unpack(projected[...]),
        precision=HIGH,
        preferred_element_type=jnp.float32,
    )
    rayleigh[...] = full
    flipped = full.T.astype(jnp.bfloat16)
    for c in range(trial.shape[0]):
        fit = jnp.dot(flipped, trial[c], preferred_element_type=jnp.float32)
        residual[c] = (image[c].astype(jnp.float32) - fit).astype(jnp.bfloat16)


def call(kernel, name, shapes, specs, *operands, scratch=(), limit=40):
    several = isinstance(shapes, tuple)
    return pl.pallas_call(
        kernel,
        out_shape=shapes,
        in_specs=specs,
        out_specs=(VMEM,) * len(shapes) if several else VMEM,
        scratch_shapes=scratch,
        compiler_params=pltpu.CompilerParams(vmem_limit_bytes=limit * MIB),
        name=name,
    )(*operands)


def f32(*shape):
    return jax.ShapeDtypeStruct(shape, jnp.float32)


def bf16(*shape):
    return jax.ShapeDtypeStruct(shape, jnp.bfloat16)


def lookup(table, wanted_ids):
    match = wanted_ids[:, None] == jnp.arange(table.shape[0], dtype=jnp.int32)[None, :]
    return jnp.sum(jnp.where(match, table[None, :], 0), axis=1)


def body(trial, band, band_width, energies, coupling, reach, pair_target, pair_source, chan_slot):
    vecs, slots, slab = trial.shape
    ys, xs, cores, slabs = (lax.axis_size(a) for a in ("y", "x", "core", "rad"))
    me = (lax.axis_index("y") * xs + lax.axis_index("x")) * cores + lax.axis_index("core")
    columns = xs * cores

    source_slot = lookup(chan_slot, pair_source)
    target_local = lookup(chan_slot, pair_target) - me * slots
    group = source_slot // slots
    member = source_slot - group * slots
    hit = group[:, None] == jnp.arange(ys * columns, dtype=jnp.int32)[None, :]
    need = jnp.sum(jnp.where(hit, member[:, None], 0), axis=0)
    needed = lax.all_gather(need, INNER)
    slot = lax.rem(group, columns) * ys + group // columns

    by_slot = jnp.transpose(trial, (1, 0, 2))
    column = lax.all_to_all(
        jnp.broadcast_to(by_slot[None], (ys,) + by_slot.shape), "y", 0, 0, tiled=True
    ).reshape(ys * slots, vecs, slab)

    up = [(i, i + 1) for i in range(slabs - 1)]
    before = lax.ppermute(by_slot[:, :, slab - BW :], "rad", up)
    after = lax.ppermute(by_slot[:, :, :BW], "rad", [(j, i) for i, j in up])
    padded = jnp.concatenate([before, by_slot, after], axis=2)
    banded = energies[:, None, None] * by_slot.astype(jnp.float32)
    for offset in range(2 * BW + 1):
        inside = (abs(offset - BW) <= band_width).astype(jnp.float32)
        weight = inside[:, None] * band[:, offset, :].astype(jnp.float32)
        banded += weight[:, None] * padded[:, :, offset : offset + slab].astype(jnp.float32)

    column, banded = lax.optimization_barrier((column, banded))
    mine = (lax.axis_index("x") * cores + lax.axis_index("core")).reshape(1)
    picked = call(
        pick_kernel, "pick", pltpu.HBM((columns * ys, vecs, slab), jnp.bfloat16), [SMEM, SMEM, VMEM], mine, needed, column
    )
    column, picked = lax.optimization_barrier((column, picked))
    rows = lax.all_to_all(picked, INNER, 0, 0, tiled=True)
    half = vecs // 2
    gram = call(gram_kernel, "gram", f32(half, 2 * vecs), [VMEM], column)
    gram = lax.dynamic_slice_in_dim(gram, lax.axis_index("y") * (half // ys), half // ys)
    gram = lax.psum(lax.psum(gram, "core"), "rad")
    rows, gram = lax.optimization_barrier((rows, gram))

    image, sent = call(
        image_kernel,
        "image",
        (bf16(*by_slot.shape), f32(half, 2 * vecs)),
        [SMEM] * 3 + [VMEM, ANY] + [VMEM] * 2,
        slot,
        target_local,
        (lax.axis_index("rad") < reach).astype(jnp.float32),
        rows,
        coupling,
        banded,
        by_slot,
        scratch=[
            pltpu.VMEM(by_slot.shape, jnp.float32),
            pltpu.VMEM(coupling.shape, jnp.bfloat16),
            pltpu.SemaphoreType.DMA((coupling.shape[0] // CHUNK,)),
        ],
        limit=50,
    )
    shared = cores * slabs
    piece = half // shared
    sent = sent.reshape(shared, piece, 2 * vecs)
    received = lax.all_to_all(sent, ("core", "rad"), 0, 0, tiled=True)
    spread = call(
        middle_kernel,
        "middle",
        f32(ys * xs, half // ys + piece, 2 * vecs),
        [VMEM, VMEM],
        received,
        gram,
    )
    received = lax.all_to_all(spread, ("y", "x"), 0, 0, tiled=True)
    spread, gram = call(
        last_kernel, "last", (f32(shared, piece, 2 * vecs), f32(vecs, vecs)), [VMEM], received
    )
    inverse = call(inverse_kernel, "inverse", f32(vecs, vecs), [VMEM], gram)
    projected = lax.all_to_all(spread, ("core", "rad"), 0, 0, tiled=True).reshape(half, 2 * vecs)
    residual, rayleigh = call(
        residual_kernel,
        "residual",
        (bf16(*by_slot.shape), f32(vecs, vecs)),
        [VMEM] * 4,
        inverse,
        projected,
        by_slot,
        image,
    )
    return jnp.transpose(residual, (1, 0, 2)), rayleigh


def solution(mesh):
    chan, rad = mesh.shape["chan"], mesh.shape["rad"]
    fine = Mesh(
        mesh.devices.reshape(chan // (X_CHIPS * CORES), X_CHIPS, CORES, rad),
        ("y", "x", "core", "rad"),
    )
    placed = (
        P(None, CHAN, "rad"),
        P(CHAN, None, "rad"),
        P(CHAN),
        P(CHAN),
        P(CHAN, "rad", None),
        P(CHAN),
        P(CHAN),
        P(CHAN),
        P(),
    )
    return jax.shard_map(
        body, mesh=fine, in_specs=placed, out_specs=(P(None, CHAN, "rad"), P()), check_vma=False
    )
```

```python
import functools

import jax
import jax.numpy as jnp
from jax import lax
from jax.experimental import pallas as pl
from jax.experimental.pallas import tpu as pltpu
from jax.sharding import Mesh, PartitionSpec as P

BW = 8
BLK = 256
CORES = 2
X_CHIPS = 4
CHUNK = 8
INNER = ("x", "core")
CHAN = ("y", "x", "core")
VMEM = pl.BlockSpec(memory_space=pltpu.VMEM)
ANY = pl.BlockSpec(memory_space=pl.ANY)
SMEM = pl.BlockSpec(memory_space=pltpu.SMEM)
NT = (((1,), (1,)), ((), ()))
HIGH = lax.Precision.HIGHEST
MIB = 1024 * 1024


def pack(square):
    half = square.shape[0] // 2
    return jnp.concatenate([square[:half], square[half:]], axis=1)


def unpack(packed):
    half = packed.shape[1] // 2
    return jnp.concatenate([packed[:, :half], packed[:, half:]], axis=0)


def gram_of(rows):
    acc = None
    for c in range(rows.shape[0]):
        term = lax.dot_general(rows[c], rows[c], NT, preferred_element_type=jnp.float32)
        acc = term if acc is None else acc + term
    return acc


def pick_kernel(mine, need, rows, out):
    receivers = need.shape[0]
    groups = out.shape[0] // receivers
    per_group = rows.shape[0] // groups
    columns = need.shape[1] // groups

    @pl.loop(0, receivers)
    def _(receiver):
        for group in range(groups):
            chosen = group * per_group + need[receiver, group * columns + mine[0]]
            out[receiver * groups + group] = rows[chosen]


def gram_kernel(rows, gram):
    gram[...] = pack(gram_of(rows))


def inverse_kernel(square, inverse):
    size = square.shape[0]
    down = lax.broadcasted_iota(jnp.int32, (size, size), 0)
    across = lax.broadcasted_iota(jnp.int32, (size, size), 1)
    value = square[...]
    for k in range(size):
        scale = 1.0 / value[k : k + 1, k : k + 1]
        row = jnp.where(across[:1] == k, 1.0, value[k : k + 1]) * scale
        column = jnp.where(down[:, :1] == k, -1.0, value[:, k : k + 1])
        rest = jnp.where((down == k) | (across == k), 0.0, value)
        value = rest - column * row
    inverse[...] = value


def image_kernel(
    slot, target, live, rows, coupling, banded, trial, image, sent, total, held, sems
):
    def copy(chunk):
        part = pl.ds(chunk * CHUNK, CHUNK)
        return pltpu.make_async_copy(coupling.at[part], held.at[part], sems.at[chunk])

    for chunk in range(sems.shape[0]):
        copy(chunk).start()
    total[...] = banded[...]

    for p in range(coupling.shape[0]):
        if p % CHUNK == 0:
            copy(p // CHUNK).wait()
        part = lax.dot_general(rows[slot[p]], held[p], NT, preferred_element_type=jnp.float32)
        total[target[p]] += part * live[p]

    acc = jnp.zeros((trial.shape[1], trial.shape[1]), jnp.float32)
    for c in range(total.shape[0]):
        rounded = total[c].astype(jnp.bfloat16)
        image[c] = rounded
        acc += lax.dot_general(trial[c], rounded, NT, preferred_element_type=jnp.float32)
    sent[...] = pack(acc)


def middle_kernel(received, gram, spread):
    whole = jnp.concatenate([gram[...], jnp.sum(received[...], axis=0)], axis=0)
    width = spread.shape[1]
    count = whole.shape[0] // width
    for j in range(spread.shape[0]):
        spread[j] = whole[j % count * width : (j % count + 1) * width]


def last_kernel(over_y, over_x, received, spread, gram):
    count = received.shape[0] // (over_y * over_x)

    def added(number, senders):
        first = received[senders[0] * count + number]
        for sender in senders[1:]:
            first += received[sender * count + number]
        return first

    whole = added(count - 1, range(over_y * over_x))
    for j in range(spread.shape[0]):
        spread[j] = whole
    found = []
    for y in range(over_y):
        for number in range(count - 1):
            found.append(added(number, range(y * over_x, (y + 1) * over_x)))
    gram[...] = unpack(jnp.concatenate(found, axis=0))


def residual_kernel(inverse, projected, trial, image, residual, rayleigh):
    full = jnp.dot(
        inverse[...],
        unpack(projected[...]),
        precision=HIGH,
        preferred_element_type=jnp.float32,
    )
    rayleigh[...] = full
    flipped = full.T.astype(jnp.bfloat16)
    for c in range(trial.shape[0]):
        fit = jnp.dot(flipped, trial[c], preferred_element_type=jnp.float32)
        residual[c] = (image[c].astype(jnp.float32) - fit).astype(jnp.bfloat16)


def call(kernel, name, shapes, specs, *operands, scratch=(), limit=40):
    several = isinstance(shapes, tuple)
    return pl.pallas_call(
        kernel,
        out_shape=shapes,
        in_specs=specs,
        out_specs=(VMEM,) * len(shapes) if several else VMEM,
        scratch_shapes=scratch,
        compiler_params=pltpu.CompilerParams(vmem_limit_bytes=limit * MIB),
        name=name,
    )(*operands)


def f32(*shape):
    return jax.ShapeDtypeStruct(shape, jnp.float32)


def bf16(*shape):
    return jax.ShapeDtypeStruct(shape, jnp.bfloat16)


def lookup(table, wanted_ids):
    match = wanted_ids[:, None] == jnp.arange(table.shape[0], dtype=jnp.int32)[None, :]
    return jnp.sum(jnp.where(match, table[None, :], 0), axis=1)


def body(trial, band, band_width, energies, coupling, reach, pair_target, pair_source, chan_slot):
    vecs, slots, slab = trial.shape
    ys, xs, cores, slabs = (lax.axis_size(a) for a in ("y", "x", "core", "rad"))
    me = (lax.axis_index("y") * xs + lax.axis_index("x")) * cores + lax.axis_index("core")
    columns = xs * cores

    source_slot = lookup(chan_slot, pair_source)
    target_local = lookup(chan_slot, pair_target) - me * slots
    group = source_slot // slots
    member = source_slot - group * slots
    hit = group[:, None] == jnp.arange(ys * columns, dtype=jnp.int32)[None, :]
    need = jnp.sum(jnp.where(hit, member[:, None], 0), axis=0)
    needed = lax.all_gather(need, INNER)
    slot = lax.rem(group, columns) * ys + group // columns

    by_slot = jnp.transpose(trial, (1, 0, 2))
    column = lax.all_to_all(
        jnp.broadcast_to(by_slot[None], (ys,) + by_slot.shape), "y", 0, 0, tiled=True
    ).reshape(ys * slots, vecs, slab)

    up = [(i, i + 1) for i in range(slabs - 1)]
    before = lax.ppermute(by_slot[:, :, slab - BW :], "rad", up)
    after = lax.ppermute(by_slot[:, :, :BW], "rad", [(j, i) for i, j in up])
    padded = jnp.concatenate([before, by_slot, after], axis=2)
    banded = energies[:, None, None] * by_slot.astype(jnp.float32)
    for offset in range(2 * BW + 1):
        inside = (abs(offset - BW) <= band_width).astype(jnp.float32)
        weight = inside[:, None] * band[:, offset, :].astype(jnp.float32)
        banded += weight[:, None] * padded[:, :, offset : offset + slab].astype(jnp.float32)

    column, banded = lax.optimization_barrier((column, banded))
    mine = (lax.axis_index("x") * cores + lax.axis_index("core")).reshape(1)
    picked = call(
        pick_kernel, "pick", bf16(columns * ys, vecs, slab), [SMEM, SMEM, VMEM], mine, needed, column
    )
    column, picked = lax.optimization_barrier((column, picked))
    rows = lax.all_to_all(picked, INNER, 0, 0, tiled=True)
    half = vecs // 2
    gram = call(gram_kernel, "gram", f32(half, 2 * vecs), [VMEM], column)
    gram = lax.dynamic_slice_in_dim(gram, lax.axis_index("y") * (half // ys), half // ys)
    gram = lax.psum(lax.psum(gram, "core"), "rad")
    rows, gram = lax.optimization_barrier((rows, gram))

    image, sent = call(
        image_kernel,
        "image",
        (bf16(*by_slot.shape), f32(half, 2 * vecs)),
        [SMEM] * 3 + [VMEM, ANY] + [VMEM] * 2,
        slot,
        target_local,
        (lax.axis_index("rad") < reach).astype(jnp.float32),
        rows,
        coupling,
        banded,
        by_slot,
        scratch=[
            pltpu.VMEM(by_slot.shape, jnp.float32),
            pltpu.VMEM(coupling.shape, jnp.bfloat16),
            pltpu.SemaphoreType.DMA((coupling.shape[0] // CHUNK,)),
        ],
        limit=50,
    )
    shared = cores * slabs
    piece = half // shared
    sent = sent.reshape(shared, piece, 2 * vecs)
    received = lax.all_to_all(sent, ("core", "rad"), 0, 0, tiled=True)
    spread = call(
        middle_kernel,
        "middle",
        f32(ys * xs * (half // ys // piece + 1), piece, 2 * vecs),
        [VMEM, VMEM],
        received,
        gram,
    )
    received = lax.all_to_all(spread, ("y", "x"), 0, 0, tiled=True)
    spread, gram = call(
        functools.partial(last_kernel, ys, xs), "last", (f32(shared, piece, 2 * vecs), f32(vecs, vecs)), [VMEM], received
    )
    inverse = call(inverse_kernel, "inverse", f32(vecs, vecs), [VMEM], gram)
    projected = lax.all_to_all(spread, ("core", "rad"), 0, 0, tiled=True).reshape(half, 2 * vecs)
    residual, rayleigh = call(
        residual_kernel,
        "residual",
        (bf16(*by_slot.shape), f32(vecs, vecs)),
        [VMEM] * 4,
        inverse,
        projected,
        by_slot,
        image,
    )
    return jnp.transpose(residual, (1, 0, 2)), rayleigh


def solution(mesh):
    chan, rad = mesh.shape["chan"], mesh.shape["rad"]
    fine = Mesh(
        mesh.devices.reshape(chan // (X_CHIPS * CORES), X_CHIPS, CORES, rad),
        ("y", "x", "core", "rad"),
    )
    placed = (
        P(None, CHAN, "rad"),
        P(CHAN, None, "rad"),
        P(CHAN),
        P(CHAN),
        P(CHAN, "rad", None),
        P(CHAN),
        P(CHAN),
        P(CHAN),
        P(),
    )
    return jax.shard_map(
        body, mesh=fine, in_specs=placed, out_specs=(P(None, CHAN, "rad"), P()), check_vma=False
    )
```

```python
import functools

import jax
import jax.numpy as jnp
from jax import lax
from jax.experimental import pallas as pl
from jax.experimental.pallas import tpu as pltpu
from jax.sharding import Mesh, PartitionSpec as P

BW = 8
BLK = 256
CORES = 2
X_CHIPS = 4
INNER = ("x", "core")
CHAN = ("y", "x", "core")
VMEM = pl.BlockSpec(memory_space=pltpu.VMEM)
ANY = pl.BlockSpec(memory_space=pl.ANY)
SMEM = pl.BlockSpec(memory_space=pltpu.SMEM)
NT = (((1,), (1,)), ((), ()))
HIGH = lax.Precision.HIGHEST
MIB = 1024 * 1024


def pack(square):
    half = square.shape[0] // 2
    return jnp.concatenate([square[:half], square[half:]], axis=1)


def unpack(packed):
    half = packed.shape[1] // 2
    return jnp.concatenate([packed[:, :half], packed[:, half:]], axis=0)


def gram_of(rows):
    acc = None
    for c in range(rows.shape[0]):
        term = lax.dot_general(rows[c], rows[c], NT, preferred_element_type=jnp.float32)
        acc = term if acc is None else acc + term
    return acc


def pick_kernel(mine, need, rows, out, held, sems):
    receivers = need.shape[0]
    groups = out.shape[0] // receivers
    per_group = rows.shape[0] // groups
    columns = need.shape[1] // groups

    def copy(receiver):
        part = pl.ds(receiver * groups, groups)
        return pltpu.make_async_copy(held.at[part], out.at[part], sems.at[receiver])

    for receiver in range(receivers):
        for group in range(groups):
            chosen = group * per_group + need[receiver, group * columns + mine[0]]
            held[receiver * groups + group] = rows[chosen]
        copy(receiver).start()
    for receiver in range(receivers):
        copy(receiver).wait()


def gram_kernel(rows, gram):
    gram[...] = pack(gram_of(rows))


def inverse_kernel(square, inverse):
    size = square.shape[0]
    down = lax.broadcasted_iota(jnp.int32, (size, size), 0)
    across = lax.broadcasted_iota(jnp.int32, (size, size), 1)
    value = square[...]
    for k in range(size):
        scale = 1.0 / value[k : k + 1, k : k + 1]
        row = jnp.where(across[:1] == k, 1.0, value[k : k + 1]) * scale
        column = jnp.where(down[:, :1] == k, -1.0, value[:, k : k + 1])
        rest = jnp.where((down == k) | (across == k), 0.0, value)
        value = rest - column * row
    inverse[...] = value


def chunk_starts(pairs):
    return [0] + sorted({pairs * part // 16 for part in (6, 11, 14)} - {0}) + [pairs]


def image_kernel(
    slot, target, live, rows, coupling, banded, trial, image, sent, total, held, sems
):
    starts = chunk_starts(coupling.shape[0])
    copies = {}
    for i, first in enumerate(starts[:-1]):
        part = pl.ds(first, starts[i + 1] - first)
        copies[first] = pltpu.make_async_copy(coupling.at[part], held.at[part], sems.at[i])
        copies[first].start()
    total[...] = banded[...]

    for p in range(coupling.shape[0]):
        if p in copies:
            copies[p].wait()
        part = lax.dot_general(rows[slot[p]], held[p], NT, preferred_element_type=jnp.float32)
        total[target[p]] += part * live[p]

    acc = jnp.zeros((trial.shape[1], trial.shape[1]), jnp.float32)
    for c in range(total.shape[0]):
        rounded = total[c].astype(jnp.bfloat16)
        image[c] = rounded
        acc += lax.dot_general(trial[c], rounded, NT, preferred_element_type=jnp.float32)
    sent[...] = pack(acc)


def middle_kernel(received, gram, spread):
    whole = jnp.concatenate([gram[...], jnp.sum(received[...], axis=0)], axis=0)
    width = spread.shape[1]
    count = whole.shape[0] // width
    for j in range(spread.shape[0]):
        spread[j] = whole[j % count * width : (j % count + 1) * width]


def last_kernel(over_y, over_x, received, spread, gram):
    count = received.shape[0] // (over_y * over_x)

    def added(number, senders):
        first = received[senders[0] * count + number]
        for sender in senders[1:]:
            first += received[sender * count + number]
        return first

    whole = added(count - 1, range(over_y * over_x))
    for j in range(spread.shape[0]):
        spread[j] = whole
    found = []
    for y in range(over_y):
        for number in range(count - 1):
            found.append(added(number, range(y * over_x, (y + 1) * over_x)))
    gram[...] = unpack(jnp.concatenate(found, axis=0))


def residual_kernel(inverse, projected, trial, image, residual, rayleigh):
    full = jnp.dot(
        inverse[...],
        unpack(projected[...]),
        precision=HIGH,
        preferred_element_type=jnp.float32,
    )
    rayleigh[...] = full
    flipped = full.T.astype(jnp.bfloat16)
    for c in range(trial.shape[0]):
        fit = jnp.dot(flipped, trial[c], preferred_element_type=jnp.float32)
        residual[c] = (image[c].astype(jnp.float32) - fit).astype(jnp.bfloat16)


def call(kernel, name, shapes, specs, *operands, scratch=(), limit=40):
    several = isinstance(shapes, tuple)
    return pl.pallas_call(
        kernel,
        out_shape=shapes,
        in_specs=specs,
        out_specs=(VMEM,) * len(shapes) if several else VMEM,
        scratch_shapes=scratch,
        compiler_params=pltpu.CompilerParams(vmem_limit_bytes=limit * MIB),
        name=name,
    )(*operands)


def f32(*shape):
    return jax.ShapeDtypeStruct(shape, jnp.float32)


def bf16(*shape):
    return jax.ShapeDtypeStruct(shape, jnp.bfloat16)


def lookup(table, wanted_ids):
    match = wanted_ids[:, None] == jnp.arange(table.shape[0], dtype=jnp.int32)[None, :]
    return jnp.sum(jnp.where(match, table[None, :], 0), axis=1)


def body(trial, band, band_width, energies, coupling, reach, pair_target, pair_source, chan_slot):
    vecs, slots, slab = trial.shape
    ys, xs, cores, slabs = (lax.axis_size(a) for a in ("y", "x", "core", "rad"))
    me = (lax.axis_index("y") * xs + lax.axis_index("x")) * cores + lax.axis_index("core")
    columns = xs * cores

    source_slot = lookup(chan_slot, pair_source)
    target_local = lookup(chan_slot, pair_target) - me * slots
    group = source_slot // slots
    member = source_slot - group * slots
    hit = group[:, None] == jnp.arange(ys * columns, dtype=jnp.int32)[None, :]
    need = jnp.sum(jnp.where(hit, member[:, None], 0), axis=0)
    needed = lax.all_gather(need, INNER)
    slot = lax.rem(group, columns) * ys + group // columns

    by_slot = jnp.transpose(trial, (1, 0, 2))
    column = lax.all_to_all(
        jnp.broadcast_to(by_slot[None], (ys,) + by_slot.shape), "y", 0, 0, tiled=True
    ).reshape(ys * slots, vecs, slab)

    up = [(i, i + 1) for i in range(slabs - 1)]
    before = lax.ppermute(by_slot[:, :, slab - BW :], "rad", up)
    after = lax.ppermute(by_slot[:, :, :BW], "rad", [(j, i) for i, j in up])
    padded = jnp.concatenate([before, by_slot, after], axis=2)
    banded = energies[:, None, None] * by_slot.astype(jnp.float32)
    for offset in range(2 * BW + 1):
        inside = (abs(offset - BW) <= band_width).astype(jnp.float32)
        weight = inside[:, None] * band[:, offset, :].astype(jnp.float32)
        banded += weight[:, None] * padded[:, :, offset : offset + slab].astype(jnp.float32)

    column, banded = lax.optimization_barrier((column, banded))
    mine = (lax.axis_index("x") * cores + lax.axis_index("core")).reshape(1)
    picked = pl.pallas_call(
        pick_kernel,
        out_shape=pltpu.HBM((columns * ys, vecs, slab), jnp.bfloat16),
        in_specs=[SMEM, SMEM, VMEM],
        out_specs=ANY,
        scratch_shapes=[
            pltpu.VMEM((columns * ys, vecs, slab), jnp.bfloat16),
            pltpu.SemaphoreType.DMA((columns,)),
        ],
        compiler_params=pltpu.CompilerParams(vmem_limit_bytes=40 * MIB),
        name="pick",
    )(mine, needed, column)
    column, picked = lax.optimization_barrier((column, picked))
    rows = lax.all_to_all(picked, INNER, 0, 0, tiled=True)
    half = vecs // 2
    gram = call(gram_kernel, "gram", f32(half, 2 * vecs), [VMEM], column)
    gram = lax.dynamic_slice_in_dim(gram, lax.axis_index("y") * (half // ys), half // ys)
    gram = lax.psum(lax.psum(gram, "core"), "rad")
    rows, gram = lax.optimization_barrier((rows, gram))

    image, sent = call(
        image_kernel,
        "image",
        (bf16(*by_slot.shape), f32(half, 2 * vecs)),
        [SMEM] * 3 + [VMEM, ANY] + [VMEM] * 2,
        slot,
        target_local,
        (lax.axis_index("rad") < reach).astype(jnp.float32),
        rows,
        coupling,
        banded,
        by_slot,
        scratch=[
            pltpu.VMEM(by_slot.shape, jnp.float32),
            pltpu.VMEM(coupling.shape, jnp.bfloat16),
            pltpu.SemaphoreType.DMA((len(chunk_starts(coupling.shape[0])) - 1,)),
        ],
        limit=50,
    )
    shared = cores * slabs
    piece = half // shared
    sent = sent.reshape(shared, piece, 2 * vecs)
    received = lax.all_to_all(sent, ("core", "rad"), 0, 0, tiled=True)
    spread = call(
        middle_kernel,
        "middle",
        f32(ys * xs * (half // ys // piece + 1), piece, 2 * vecs),
        [VMEM, VMEM],
        received,
        gram,
    )
    received = lax.all_to_all(spread, ("y", "x"), 0, 0, tiled=True)
    spread, gram = call(
        functools.partial(last_kernel, ys, xs), "last", (f32(shared, piece, 2 * vecs), f32(vecs, vecs)), [VMEM], received
    )
    inverse = call(inverse_kernel, "inverse", f32(vecs, vecs), [VMEM], gram)
    projected = lax.all_to_all(spread, ("core", "rad"), 0, 0, tiled=True).reshape(half, 2 * vecs)
    residual, rayleigh = call(
        residual_kernel,
        "residual",
        (bf16(*by_slot.shape), f32(vecs, vecs)),
        [VMEM] * 4,
        inverse,
        projected,
        by_slot,
        image,
    )
    return jnp.transpose(residual, (1, 0, 2)), rayleigh


def solution(mesh):
    chan, rad = mesh.shape["chan"], mesh.shape["rad"]
    fine = Mesh(
        mesh.devices.reshape(chan // (X_CHIPS * CORES), X_CHIPS, CORES, rad),
        ("y", "x", "core", "rad"),
    )
    placed = (
        P(None, CHAN, "rad"),
        P(CHAN, None, "rad"),
        P(CHAN),
        P(CHAN),
        P(CHAN, "rad", None),
        P(CHAN),
        P(CHAN),
        P(CHAN),
        P(),
    )
    return jax.shard_map(
        body, mesh=fine, in_specs=placed, out_specs=(P(None, CHAN, "rad"), P()), check_vma=False
    )
```

```python
import functools

import jax
import jax.numpy as jnp
from jax import lax
from jax.experimental import pallas as pl
from jax.experimental.pallas import tpu as pltpu
from jax.sharding import Mesh, PartitionSpec as P

BW = 8
BLK = 256
CORES = 2
X_CHIPS = 4
CHUNK = 8
INNER = ("x", "core")
CHAN = ("y", "x", "core")
VMEM = pl.BlockSpec(memory_space=pltpu.VMEM)
ANY = pl.BlockSpec(memory_space=pl.ANY)
SMEM = pl.BlockSpec(memory_space=pltpu.SMEM)
NT = (((1,), (1,)), ((), ()))
HIGH = lax.Precision.HIGHEST
MIB = 1024 * 1024


def pack(square):
    half = square.shape[0] // 2
    return jnp.concatenate([square[:half], square[half:]], axis=1)


def unpack(packed):
    half = packed.shape[1] // 2
    return jnp.concatenate([packed[:, :half], packed[:, half:]], axis=0)


def gram_of(rows):
    acc = None
    for c in range(rows.shape[0]):
        term = lax.dot_general(rows[c], rows[c], NT, preferred_element_type=jnp.float32)
        acc = term if acc is None else acc + term
    return acc


def pick_kernel(mine, need, rows, out, held, sems):
    receivers = need.shape[0]
    groups = out.shape[0] // receivers
    per_group = rows.shape[0] // groups
    columns = need.shape[1] // groups

    def copy(receiver):
        part = pl.ds(receiver * groups, groups)
        return pltpu.make_async_copy(held.at[part], out.at[part], sems.at[receiver])

    for receiver in range(receivers):
        for group in range(groups):
            chosen = group * per_group + need[receiver, group * columns + mine[0]]
            held[receiver * groups + group] = rows[chosen]
        copy(receiver).start()
    for receiver in range(receivers):
        copy(receiver).wait()


def gram_kernel(rows, gram):
    gram[...] = pack(gram_of(rows))


def inverse_kernel(square, inverse):
    size = square.shape[0]
    down = lax.broadcasted_iota(jnp.int32, (size, size), 0)
    across = lax.broadcasted_iota(jnp.int32, (size, size), 1)
    value = square[...]
    for k in range(size):
        scale = 1.0 / value[k : k + 1, k : k + 1]
        row = jnp.where(across[:1] == k, 1.0, value[k : k + 1]) * scale
        column = jnp.where(down[:, :1] == k, -1.0, value[:, k : k + 1])
        rest = jnp.where((down == k) | (across == k), 0.0, value)
        value = rest - column * row
    inverse[...] = value


def image_kernel(
    slot, target, live, rows, coupling, banded, trial, image, sent, total, held, sems
):
    def copy(chunk):
        part = pl.ds(chunk * CHUNK, CHUNK)
        return pltpu.make_async_copy(coupling.at[part], held.at[part], sems.at[chunk])

    for chunk in range(sems.shape[0]):
        copy(chunk).start()
    total[...] = banded[...]

    for p in range(coupling.shape[0]):
        if p % CHUNK == 0:
            copy(p // CHUNK).wait()
        part = lax.dot_general(rows[slot[p]], held[p], NT, preferred_element_type=jnp.float32)
        total[target[p]] += part * live[p]

    acc = jnp.zeros((trial.shape[1], trial.shape[1]), jnp.float32)
    for c in range(total.shape[0]):
        rounded = total[c].astype(jnp.bfloat16)
        image[c] = rounded
        acc += lax.dot_general(trial[c], rounded, NT, preferred_element_type=jnp.float32)
    sent[...] = pack(acc)


def middle_kernel(received, gram, spread):
    whole = jnp.concatenate([gram[...], jnp.sum(received[...], axis=0)], axis=0)
    width = spread.shape[1]
    count = whole.shape[0] // width
    for j in range(spread.shape[0]):
        spread[j] = whole[j % count * width : (j % count + 1) * width]


def last_kernel(over_y, over_x, received, spread, gram):
    count = received.shape[0] // (over_y * over_x)

    def added(number, senders):
        first = received[senders[0] * count + number]
        for sender in senders[1:]:
            first += received[sender * count + number]
        return first

    whole = added(count - 1, range(over_y * over_x))
    for j in range(spread.shape[0]):
        spread[j] = whole
    found = []
    for y in range(over_y):
        for number in range(count - 1):
            found.append(added(number, range(y * over_x, (y + 1) * over_x)))
    gram[...] = unpack(jnp.concatenate(found, axis=0))


def residual_kernel(inverse, projected, trial, image, residual, rayleigh):
    full = jnp.dot(
        inverse[...],
        unpack(projected[...]),
        precision=HIGH,
        preferred_element_type=jnp.float32,
    )
    rayleigh[...] = full
    flipped = full.T.astype(jnp.bfloat16)
    for c in range(trial.shape[0]):
        fit = jnp.dot(flipped, trial[c], preferred_element_type=jnp.float32)
        residual[c] = (image[c].astype(jnp.float32) - fit).astype(jnp.bfloat16)


def call(kernel, name, shapes, specs, *operands, scratch=(), limit=40):
    several = isinstance(shapes, tuple)
    return pl.pallas_call(
        kernel,
        out_shape=shapes,
        in_specs=specs,
        out_specs=(VMEM,) * len(shapes) if several else VMEM,
        scratch_shapes=scratch,
        compiler_params=pltpu.CompilerParams(vmem_limit_bytes=limit * MIB),
        name=name,
    )(*operands)


def f32(*shape):
    return jax.ShapeDtypeStruct(shape, jnp.float32)


def bf16(*shape):
    return jax.ShapeDtypeStruct(shape, jnp.bfloat16)


def lookup(table, wanted_ids):
    match = wanted_ids[:, None] == jnp.arange(table.shape[0], dtype=jnp.int32)[None, :]
    return jnp.sum(jnp.where(match, table[None, :], 0), axis=1)


def body(trial, band, band_width, energies, coupling, reach, pair_target, pair_source, chan_slot):
    vecs, slots, slab = trial.shape
    ys, xs, cores, slabs = (lax.axis_size(a) for a in ("y", "x", "core", "rad"))
    me = (lax.axis_index("y") * xs + lax.axis_index("x")) * cores + lax.axis_index("core")
    columns = xs * cores

    source_slot = lookup(chan_slot, pair_source)
    target_local = lookup(chan_slot, pair_target) - me * slots
    group = source_slot // slots
    member = source_slot - group * slots
    hit = group[:, None] == jnp.arange(ys * columns, dtype=jnp.int32)[None, :]
    need = jnp.sum(jnp.where(hit, member[:, None], 0), axis=0)
    needed = lax.all_gather(need, INNER)
    slot = lax.rem(group, columns) * ys + group // columns

    by_slot = jnp.transpose(trial, (1, 0, 2))
    column = lax.all_to_all(
        jnp.broadcast_to(by_slot[None], (ys,) + by_slot.shape), "y", 0, 0, tiled=True
    ).reshape(ys * slots, vecs, slab)

    up = [(i, i + 1) for i in range(slabs - 1)]
    before = lax.ppermute(by_slot[:, :, slab - BW :], "rad", up)
    after = lax.ppermute(by_slot[:, :, :BW], "rad", [(j, i) for i, j in up])
    padded = jnp.concatenate([before, by_slot, after], axis=2)
    banded = energies[:, None, None] * by_slot.astype(jnp.float32)
    for offset in range(2 * BW + 1):
        inside = (abs(offset - BW) <= band_width).astype(jnp.float32)
        weight = inside[:, None] * band[:, offset, :].astype(jnp.float32)
        banded += weight[:, None] * padded[:, :, offset : offset + slab].astype(jnp.float32)

    column, banded = lax.optimization_barrier((column, banded))
    mine = (lax.axis_index("x") * cores + lax.axis_index("core")).reshape(1)
    picked = pl.pallas_call(
        pick_kernel,
        out_shape=pltpu.HBM((columns * ys, vecs, slab), jnp.bfloat16),
        in_specs=[SMEM, SMEM, VMEM],
        out_specs=ANY,
        scratch_shapes=[
            pltpu.VMEM((columns * ys, vecs, slab), jnp.bfloat16),
            pltpu.SemaphoreType.DMA((columns,)),
        ],
        compiler_params=pltpu.CompilerParams(vmem_limit_bytes=40 * MIB),
        name="pick",
    )(mine, needed, column)
    column, picked = lax.optimization_barrier((column, picked))
    rows = lax.all_to_all(picked, INNER, 0, 0, tiled=True)
    half = vecs // 2
    gram = call(gram_kernel, "gram", f32(half, 2 * vecs), [VMEM], column)
    gram = lax.dynamic_slice_in_dim(gram, lax.axis_index("y") * (half // ys), half // ys)
    gram = lax.psum(lax.psum(gram, "core"), "rad")
    rows, gram = lax.optimization_barrier((rows, gram))

    image, sent = call(
        image_kernel,
        "image",
        (bf16(*by_slot.shape), f32(half, 2 * vecs)),
        [SMEM] * 3 + [VMEM, ANY] + [VMEM] * 2,
        slot,
        target_local,
        (lax.axis_index("rad") < reach).astype(jnp.float32),
        rows,
        coupling,
        banded,
        by_slot,
        scratch=[
            pltpu.VMEM(by_slot.shape, jnp.float32),
            pltpu.VMEM(coupling.shape, jnp.bfloat16),
            pltpu.SemaphoreType.DMA((coupling.shape[0] // CHUNK,)),
        ],
        limit=50,
    )
    shared = cores * slabs
    piece = half // shared
    sent = sent.reshape(shared, piece, 2 * vecs)
    received = lax.all_to_all(sent, ("core", "rad"), 0, 0, tiled=True)
    spread = call(
        middle_kernel,
        "middle",
        f32(ys * xs * (half // ys // piece + 1), piece, 2 * vecs),
        [VMEM, VMEM],
        received,
        gram,
    )
    received = lax.all_to_all(spread, ("y", "x"), 0, 0, tiled=True)
    spread, gram = call(
        functools.partial(last_kernel, ys, xs), "last", (f32(shared, piece, 2 * vecs), f32(vecs, vecs)), [VMEM], received
    )
    inverse = call(inverse_kernel, "inverse", f32(vecs, vecs), [VMEM], gram)
    projected = lax.all_to_all(spread, ("core", "rad"), 0, 0, tiled=True).reshape(half, 2 * vecs)
    residual, rayleigh = call(
        residual_kernel,
        "residual",
        (bf16(*by_slot.shape), f32(vecs, vecs)),
        [VMEM] * 4,
        inverse,
        projected,
        by_slot,
        image,
    )
    return jnp.transpose(residual, (1, 0, 2)), rayleigh


def solution(mesh):
    chan, rad = mesh.shape["chan"], mesh.shape["rad"]
    fine = Mesh(
        mesh.devices.reshape(chan // (X_CHIPS * CORES), X_CHIPS, CORES, rad),
        ("y", "x", "core", "rad"),
    )
    placed = (
        P(None, CHAN, "rad"),
        P(CHAN, None, "rad"),
        P(CHAN),
        P(CHAN),
        P(CHAN, "rad", None),
        P(CHAN),
        P(CHAN),
        P(CHAN),
        P(),
    )
    return jax.shard_map(
        body, mesh=fine, in_specs=placed, out_specs=(P(None, CHAN, "rad"), P()), check_vma=False
    )
```
